32 devices in a mesh: seq: 4 (over y, x), group: 8 (over z, core).
Axes of the slice: x: 2, y: 2, z: 4, core: 2. Of those that a mesh axis runs over, the one named last changes fastest.
Arguments:
- block_input: bfloat16 [4, 2048, 2048], P('seq', 'group'), may hold values from -6 to 6
- out_cotangent: bfloat16 [4, 2048, 2048], P('seq', 'group'), may hold values from -6 to 6
- norm_gain: float32 [2048], replicated, may hold values from 0.1 to 1.9
- in_weight: bfloat16 [2048, 5120], P('group'), may hold values from -0.125 to 0.125
- conv_weight: float32 [4, 2560], replicated, may hold values from -3 to 3
- conv_bias: float32 [2560], replicated, may hold values from -3 to 3
- gate_weight: bfloat16 [2, 10, 256, 256], replicated, may hold values from -0.375 to 0.375
- gate_bias: float32 [2, 2560], replicated, may hold values from -3 to 3
- decay_param: float32 [2560], replicated, as said below
- out_weight: bfloat16 [2560, 2048], P('group'), may hold values from -0.125 to 0.125
- mlp_gain: float32 [2048], replicated, may hold values from 0.1 to 1.9
- mlp_weight: bfloat16 [2048, 12288], P('group'), may hold values from -0.125 to 0.125
- down_weight: bfloat16 [6144, 2048], P('group'), may hold values from -0.078125 to 0.078125
Outputs:
- block_out: bfloat16 [4, 2048, 2048], P('seq', 'group')
- input_grad: float32 [4, 2048, 2048], P('seq', 'group')
- norm_gain_grad: float32 [2048], replicated
- in_weight_grad: float32 [2048, 5120], P('group')
- conv_weight_grad: float32 [4, 2560], replicated
- conv_bias_grad: float32 [2560], replicated
- gate_weight_grad: float32 [2, 10, 256, 256], replicated
- gate_bias_grad: float32 [2, 2560], replicated
- decay_grad: float32 [2560], replicated
- out_weight_grad: float32 [2560, 2048], P('group')
- mlp_gain_grad: float32 [2048], replicated
- mlp_weight_grad: float32 [2048, 12288], P('group')
- down_weight_grad: float32 [6144, 2048], P('group')
The draws below stay inside these ranges and needn't reach their ends.
Inputs may be any that keep to these rules, and one draw needn't show every extreme that they name: `decay_param`: softplus of every entry lies between 0.01 / 2048 and 0.03.
All inputs are finite; a program needn't handle non-finite values.
Results may differ from the reference program's by a relative error of at most 0.013.
Values may be sent and summed in bfloat16 or wider, within the bound.
No kernel may reach another device: no remote copies, remote signals or barrier semaphores. Data moves between devices by JAX's collectives and lax.ppermute only.
A program may use at most 576 MiB of HBM per device.

```python
import jax
import jax.numpy as jnp
from jax import lax

D = 2048
R = 2560
HEADS = 10
FF = 6144
CONV = 4
TOK_DEV = 256
SEQS = 4
LENGTH = 2048


def draw_decay_param(key, part):
    key = jax.random.fold_in(key, 7)
    lowest = 0.01 / LENGTH
    highest = 0.03
    rate = jnp.exp(jax.random.uniform(key, (R,), jnp.float32, jnp.log(lowest), jnp.log(highest)))
    return jnp.log(jnp.expm1(rate)).astype(jnp.float32)


def shard_levels(key, extent, pieces, low, largest):
    level = 1.0
    for position, shards_of in pieces:
        draws = jax.random.uniform(jax.random.fold_in(jax.random.fold_in(key, 6), position), (shards_of,), jnp.float32, low / len(pieces), largest / len(pieces))
        level = level * jnp.repeat(jnp.exp(draws), extent[position] // shards_of).reshape((-1,) + (1,) * (len(extent) - 1 - position))
    return level


def gaussian(key, shape, spread, bound, shards=(), dtype=jnp.bfloat16):
    values = spread * jax.random.normal(key, shape, jnp.float32)
    if shards:
        values = values * shard_levels(key, shape, shards, -0.22, 0.18)
    return jnp.clip(values, -bound, bound).astype(dtype)


def setup_inputs(seed: int = 0) -> dict:
    splits = jax.random.split(jax.random.key(seed), 14)
    block_input = gaussian(splits[0], (SEQS, LENGTH, D), 1.0, 6.0, ((0, 4), (1, 8)))
    out_cotangent = gaussian(splits[1], (SEQS, LENGTH, D), 1.0, 6.0, ((0, 4), (1, 8)))
    norm_gain = jnp.clip(1.0 + 0.18 * jax.random.normal(splits[2], (D,), jnp.float32), 0.1, 1.9)
    in_weight = gaussian(splits[3], (D, 2 * R), D ** -0.5, 0.125, ((0, 8),))
    conv_weight = gaussian(splits[4], (CONV, R), 0.5, 3.0, (), jnp.float32)
    conv_bias = gaussian(splits[5], (R,), 0.5, 3.0, (), jnp.float32)
    gate_weight = gaussian(splits[6], (2, HEADS, R // HEADS, R // HEADS), (R // HEADS) ** -0.5, 0.375)
    gate_bias = gaussian(splits[7], (2, R), 1.0, 3.0, (), jnp.float32)
    decay_param = draw_decay_param(jax.random.fold_in(splits[13], 71), 0)
    out_weight = gaussian(splits[9], (R, D), R ** -0.5, 0.125, ((0, 8),))
    mlp_gain = jnp.clip(1.0 + 0.18 * jax.random.normal(splits[10], (D,), jnp.float32), 0.1, 1.9)
    mlp_weight = gaussian(splits[11], (D, 2 * FF), D ** -0.5, 0.125, ((0, 8),))
    down_weight = gaussian(splits[12], (FF, D), FF ** -0.5, 0.078125, ((0, 8),))
    return dict(block_input=block_input, out_cotangent=out_cotangent, norm_gain=norm_gain, in_weight=in_weight, conv_weight=conv_weight, conv_bias=conv_bias, gate_weight=gate_weight, gate_bias=gate_bias, decay_param=decay_param, out_weight=out_weight, mlp_gain=mlp_gain, mlp_weight=mlp_weight, down_weight=down_weight)


epsilon = 1e-06

@jax.custom_vjp
def low(v):
    return lax.optimization_barrier(v.astype(jnp.bfloat16)).astype(jnp.float32)

@jax.custom_vjp
def low_back(v):
    return v

def low_keep(v):
    return (low(v), None)

def low_pass(kept, grad):
    return (grad,)

def back_keep(v):
    return (v, None)

def back_low(kept, grad):
    return (low(grad),)
low.defvjp(low_keep, low_pass)
low_back.defvjp(back_keep, back_low)

def product_of(left, right):
    return jnp.dot(left, right, precision=lax.Precision.HIGHEST)

def rms_piece(value, gain):
    return value * lax.rsqrt(lax.optimization_barrier(jnp.mean(value * value, axis=-1, keepdims=True)) + epsilon) * gain

def gate_piece(conv_out, gate_pre, gate_bias, decay_param):
    recur_gate = jax.nn.sigmoid(gate_pre[0] + gate_bias[0])
    input_gate = jax.nn.sigmoid(gate_pre[1] + gate_bias[1])
    log_decay = -8.0 * recur_gate * jax.nn.softplus(decay_param)
    decay = jnp.exp(log_decay)
    return (decay, conv_out * input_gate * jnp.sqrt(-jnp.expm1(2.0 * log_decay)))

def recur(decay, driven):

    def block(state, pair):

        def step(carry, terms):
            fresh = terms[0] * carry + terms[1]
            return (fresh, fresh)
        return lax.scan(step, state, pair)
    pairs = (decay.reshape(-1, TOK_DEV, R), driven.reshape(-1, TOK_DEV, R))
    _, states = lax.scan(jax.checkpoint(block), jnp.zeros((R,), jnp.float32), pairs)
    return states.reshape(-1, R)

def block_forward(inputs, norm_gain, in_weight, conv_weight, conv_bias, gate_weight, gate_bias, decay_param, out_weight, mlp_gain, mlp_weight, down_weight):
    length = inputs.shape[0]
    normed = low(rms_piece(inputs, norm_gain))
    projected = low_back(product_of(normed, in_weight))
    branch_x = projected[:, :R]
    branch_pre = projected[:, R:]
    padded = jnp.concatenate([jnp.zeros((CONV - 1, R), jnp.float32), branch_x], 0)
    conv_out = conv_bias + conv_weight[0] * padded[CONV - 1:CONV - 1 + length]
    for offset in range(1, CONV):
        conv_out = conv_out + conv_weight[offset] * padded[CONV - 1 - offset:CONV - 1 - offset + length]
    conv_low = low(conv_out).reshape(length, HEADS, R // HEADS)
    gate_pre = jnp.einsum('thk,ghkj->gthj', conv_low, gate_weight, precision=lax.Precision.HIGHEST)
    gate_pre = low_back(gate_pre.reshape(2, length, R))
    decay, driven = gate_piece(conv_out, gate_pre, gate_bias, decay_param)
    states = recur(decay, driven)
    merged = low(states * jax.nn.gelu(branch_pre))
    resid = inputs + low_back(product_of(merged, out_weight))
    normed2 = low(rms_piece(resid, mlp_gain))
    gate_up = low_back(product_of(normed2, mlp_weight))
    hidden = low(jax.nn.gelu(gate_up[:, :FF]) * gate_up[:, FF:])
    return resid + low_back(product_of(hidden, down_weight))

def reference(block_input, out_cotangent, norm_gain, in_weight, conv_weight, conv_bias, gate_weight, gate_bias, decay_param, out_weight, mlp_gain, mlp_weight, down_weight):
    params = tuple((p.astype(jnp.float32) for p in (norm_gain, in_weight, conv_weight, conv_bias, gate_weight, gate_bias, decay_param, out_weight, mlp_gain, mlp_weight, down_weight)))

    def one_sequence(totals, pair):
        inputs, cotangents = pair
        result, pull = jax.vjp(block_forward, inputs, *params)
        grads = pull(cotangents)
        totals = tuple((total + grad for total, grad in zip(totals, grads[1:])))
        return (totals, (result.astype(jnp.bfloat16), grads[0]))
    start = tuple((jnp.zeros_like(p) for p in params))
    totals, (outputs, input_grads) = lax.scan(one_sequence, start, (block_input.astype(jnp.float32), out_cotangent.astype(jnp.float32)))
    return (outputs, input_grads, totals[0], totals[1], totals[2], totals[3], totals[4], totals[5], totals[6], totals[7], totals[8], totals[9], totals[10])
```

```python
import functools

import jax
import jax.numpy as jnp
from jax import lax
from jax.experimental import pallas as pl
from jax.experimental.pallas import tpu as pltpu
from jax.sharding import PartitionSpec as P

epsilon = 1e-06
f32 = jnp.float32
bf16 = jnp.bfloat16
VMEM_LIMIT = 58 * 1024 * 1024


def swap(block, k):
    return lax.ppermute(block, "seq", [(i, i ^ k) for i in range(lax.axis_size("seq"))])


def shift(block, distance):
    devices = range(lax.axis_size("group"))
    return lax.ppermute(
        block, "group", [(i - distance, i) for i in devices if i - distance in devices]
    )


def gather_seq(block):
    half = block.shape[0] // 2
    first = swap(block, 1)
    second = swap(block, 2)
    third = jnp.concatenate([swap(first[:half], 2), swap(second[half:], 1)], 0)
    return [block, first, second, third]


def scatter_seq(parts):
    half = parts[0].shape[0] // 2
    own, first, second, third = parts
    top = swap(third[:half], 1)
    bottom = swap(third[half:], 2)
    first_top = swap(first[:half], 1)
    second_bottom = swap(second[half:], 2)
    second_top = swap((second[:half].astype(f32) + top.astype(f32)).astype(bf16), 2)
    first_bottom = swap((first[half:].astype(f32) + bottom.astype(f32)).astype(bf16), 1)
    return jnp.concatenate(
        [
            own[:half].astype(f32) + first_top.astype(f32) + second_top.astype(f32),
            own[half:].astype(f32) + first_bottom.astype(f32) + second_bottom.astype(f32),
        ],
        0,
    )


def gather_group(block):
    return lax.all_gather(block, "group", axis=0, tiled=True)


def scatter_group(block):
    return lax.psum_scatter(block, "group", scatter_dimension=0, tiled=True)


def total(value):
    for axis in ("group", "seq"):
        count = lax.axis_size(axis)
        step = 1
        while step < count:
            value = value + lax.ppermute(value, axis, [(i, i ^ step) for i in range(count)])
            step *= 2
    return value


def link(earlier, later):
    return (earlier[0] * later[0], later[1] + later[0] * earlier[1])


def entering(decay, state, sign):
    count = lax.axis_size("group")
    pair = jnp.stack([decay, state])
    pair = shift(pair, sign)
    step = 1
    while step < count:
        before = shift(pair, sign * step)
        pair = jnp.stack(link((before[0], before[1]), (pair[0], pair[1])))
        step *= 2
    return pair[1]


def rms_low(value, gain):
    scale = lax.rsqrt(jnp.mean(value * value, axis=-1, keepdims=True) + epsilon)
    return (value * scale * gain).astype(bf16)


def rms_back(value, gain, grad):
    width = value.shape[-1]
    scale = lax.rsqrt(jnp.mean(value * value, axis=-1, keepdims=True) + epsilon)
    scaled = grad * gain
    along = jnp.sum(scaled * value, axis=-1, keepdims=True) / width
    grad_value = scale * scaled - value * (scale * scale * scale * along)
    grad_gain = jnp.sum(grad * value * scale, axis=0)
    return grad_value, grad_gain


ROOT = 0.7978845608028654
CUBE = 0.044715


def gelu(v):
    return 0.5 * v * (1.0 + jnp.tanh(ROOT * (v + CUBE * v * v * v)))


def gelu_both(v):
    square = v * v
    t = jnp.tanh(ROOT * v * (1.0 + CUBE * square))
    half = 0.5 * (1.0 + t)
    slope = half + 0.5 * v * (1.0 - t * t) * (ROOT * (1.0 + 3.0 * CUBE * square))
    return v * half, slope


def one_less_square(double):
    series = jnp.full_like(double, 1.0 / 362880.0)
    for term in (40320.0, 5040.0, 720.0, 120.0, 24.0, 6.0, 2.0, 1.0):
        series = series * double + 1.0 / term
    return -double * series


def rows_of(shape):
    return lax.broadcasted_iota(jnp.int32, shape, 0)


def pick(odd, value, width):
    lanes = value.shape[-1]
    return jnp.where(odd, value[:, lanes - width :], value[:, lanes - 2 * width : lanes - width])


def forward_kernel(
    head, odd_ref, u_ref, rim_ref, cw_ref, cb_ref, gw_ref, gs_ref, gb_ref, sp_ref,
    conv_ref, recur_ref, input_ref, decay_ref, state_ref, cum_ref,
    padded, low, pre,
):
    tokens, wide = u_ref.shape[1:]
    own = recur_ref.shape[2]
    odd = odd_ref[0] == 1
    padded[0:8] = rim_ref[0]
    padded[8:] = u_ref[0]
    taps = cw_ref.shape[0]

    def convolve(index, carry):
        start = pl.multiple_of(index * 32, 32)
        window = padded[pl.ds(start, 40), :]
        out = cb_ref[...] + cw_ref[0:1] * window[8:]
        for k in range(1, taps):
            out = out + cw_ref[k : k + 1] * pltpu.roll(window, k, 0)[8:]
        conv_ref[0, pl.ds(start, 32), :] = out
        low[pl.ds(start, 32), :] = out.astype(bf16)
        return carry

    lax.fori_loop(0, tokens // 32, convolve, 0)
    for g in range(2):
        for h in range(2):
            cols = slice(h * head, (h + 1) * head)
            pre[g, :, cols] = jnp.dot(low[:, cols], gw_ref[g, h], preferred_element_type=f32)
        pre[g, :, 2 * head :] = jnp.dot(low[:, 2 * head :], gs_ref[g], preferred_element_type=f32)
    row = rows_of((8, own))

    def scan(index, carry):
        cum, state = carry
        start = pl.multiple_of(index * 16, 16)
        span = pl.ds(start, 16)
        recur = jax.nn.sigmoid(pre[0, span, :] + gb_ref[0:1])
        gate = jax.nn.sigmoid(pre[1, span, :] + gb_ref[1:2])
        log_decay = recur * sp_ref[...]
        decay = jnp.exp(log_decay)
        conv = conv_ref[0, span, :]
        conv = jnp.concatenate([conv[:, : 2 * head], pick(odd, conv, head // 2)], 1)
        driven = conv * gate * jnp.sqrt(one_less_square(2.0 * log_decay))
        recur_ref[0, span, :] = recur
        input_ref[0, span, :] = gate
        decay_ref[0, span, :] = decay
        for tile in range(2):
            a = decay[tile * 8 : tile * 8 + 8]
            b = driven[tile * 8 : tile * 8 + 8]
            for d in (1, 2, 4):
                there = row >= d
                before_a = jnp.where(there, pltpu.roll(a, d, 0), 1.0)
                before_b = jnp.where(there, pltpu.roll(b, d, 0), 0.0)
                b = b + a * before_b
                a = a * before_a
            b = b + a * state
            a = a * cum
            place = pl.ds(start + tile * 8, 8)
            state_ref[0, place, :] = b
            cum_ref[0, place, :] = a
            cum, state = a[7:8], b[7:8]
        return cum, state

    lax.fori_loop(
        0, tokens // 16, scan, (jnp.ones((1, own), f32), jnp.zeros((1, own), f32))
    )


def merge_kernel(state_ref, cum_ref, carry_ref, pre_ref, h_ref, merged_ref):
    def step(index, none):
        span = pl.ds(pl.multiple_of(index * 32, 32), 32)
        state = state_ref[0, span, :] + cum_ref[0, span, :] * carry_ref[0, 0:1]
        h_ref[0, span, :] = state
        merged_ref[0, span, :] = (state * gelu(pre_ref[0, span, :])).astype(bf16)
        return none

    lax.fori_loop(0, state_ref.shape[1] // 32, step, 0)


def adjoint_kernel(gm_ref, h_ref, pre_ref, decay_ref, gh_ref, gpre_ref, back_ref, cum_ref):
    tokens, own = gm_ref.shape[1:]
    row = rows_of((8, own))
    count = tokens // 16

    def step(index, carry):
        cum, back = carry
        start = pl.multiple_of((count - 1 - index) * 16, 16)
        span = pl.ds(start, 16)
        grad = gm_ref[0, span, :]
        act, slope = gelu_both(pre_ref[0, span, :])
        gpre_ref[0, span, :] = (grad * h_ref[0, span, :] * slope).astype(bf16)
        grad_h = grad * act
        gh_ref[0, span, :] = grad_h
        decay = decay_ref[0, span, :]
        driven = decay * grad_h
        for tile in (1, 0):
            a = decay[tile * 8 : tile * 8 + 8]
            b = driven[tile * 8 : tile * 8 + 8]
            for d in (1, 2, 4):
                there = row < 8 - d
                after_a = jnp.where(there, pltpu.roll(a, 8 - d, 0), 1.0)
                after_b = jnp.where(there, pltpu.roll(b, 8 - d, 0), 0.0)
                b = b + a * after_b
                a = a * after_a
            b = b + a * back
            a = a * cum
            place = pl.ds(start + tile * 8, 8)
            back_ref[0, place, :] = b
            cum_ref[0, place, :] = a
            cum, back = a[0:1], b[0:1]
        return cum, back

    lax.fori_loop(0, count, step, (jnp.ones((1, own), f32), jnp.zeros((1, own), f32)))


def backward_kernel(
    head, odd_ref, back_ref, cum_ref, gh_ref, h_ref, carry_ref, enter_ref, recur_ref, input_ref,
    decay_ref, conv_ref, u_ref, rim_ref, cw_ref, gw_ref, gs_ref, sp_ref,
    gu_ref, tail_ref, lead_ref, small_ref, taps_ref, gwg_ref, gsg_ref,
    padded, ahead, behind, low, gg, direct,
):
    tokens, wide = u_ref.shape[1:]
    own = recur_ref.shape[2]
    half = head // 2
    odd = odd_ref[0] == 1
    taps = cw_ref.shape[0]

    @pl.when(pl.program_id(0) == 0)
    def _():
        small_ref[...] = jnp.zeros_like(small_ref)
        taps_ref[...] = jnp.zeros_like(taps_ref)
        gwg_ref[...] = jnp.zeros_like(gwg_ref)
        gsg_ref[...] = jnp.zeros_like(gsg_ref)

    padded[0:8] = rim_ref[0]
    padded[8:] = u_ref[0]
    behind[0:8] = carry_ref[0]
    ahead[tokens:] = enter_ref[0]
    direct[tokens:] = jnp.zeros((8, wide), f32)
    enter = enter_ref[0, 0:1]

    def prepare(index, none):
        start = pl.multiple_of(index * 32, 32)
        span = pl.ds(start, 32)
        ahead[span, :] = back_ref[0, span, :] + cum_ref[0, span, :] * enter
        behind[pl.ds(start + 8, 32), :] = h_ref[0, span, :]
        return none

    lax.fori_loop(0, tokens // 32, prepare, 0)

    def gates(index, sums):
        sum_recur, sum_input, sum_decay = sums
        start = pl.multiple_of(index * 16, 16)
        span = pl.ds(start, 16)
        after = pltpu.roll(ahead[pl.ds(start, 24), :], 23, 0)[:16]
        before = pltpu.roll(behind[pl.ds(start, 24), :], 1, 0)[8:]
        adj = gh_ref[0, span, :] + after
        recur = recur_ref[0, span, :]
        gate = input_ref[0, span, :]
        decay = decay_ref[0, span, :]
        whole = conv_ref[0, span, :]
        low[span, :] = whole.astype(bf16)
        conv = jnp.concatenate([whole[:, : 2 * head], pick(odd, whole, half)], 1)
        square = one_less_square(2.0 * (recur * sp_ref[...]))
        inverse = lax.rsqrt(square)
        root = square * inverse
        grad_a = adj * before
        part = adj * gate
        grad_direct = part * root
        grad_gate = adj * conv * root
        grad_root = part * conv
        grad_log = decay * (grad_a - grad_root * decay * inverse)
        scaled = grad_log * recur
        grad_recur = scaled * sp_ref[...] * (1.0 - recur)
        grad_input = grad_gate * gate * (1.0 - gate)
        gg[0, span, :] = grad_recur.astype(bf16)
        gg[1, span, :] = grad_input.astype(bf16)
        shared = grad_direct[:, 2 * head :]
        none = jnp.zeros_like(shared)
        direct[span, :] = jnp.concatenate(
            [grad_direct[:, : 2 * head], jnp.where(odd, none, shared), jnp.where(odd, shared, none)],
            1,
        )
        fold = lambda old, new: old + new[:8] + new[8:]
        return fold(sum_recur, grad_recur), fold(sum_input, grad_input), fold(sum_decay, scaled)

    zero = jnp.zeros((8, own), f32)
    sums = lax.fori_loop(0, tokens // 16, gates, (zero, zero, zero))
    for position, value in enumerate(sums):
        small_ref[position : position + 1] += jnp.sum(value, axis=0, keepdims=True)
    across = (((1,), (1,)), ((), ()))
    down = (((0,), (0,)), ((), ()))
    for h in range(2):
        cols = slice(h * head, (h + 1) * head)
        direct[0:tokens, cols] += lax.dot_general(
            gg[0, :, cols], gw_ref[0, h], across, preferred_element_type=f32
        ) + lax.dot_general(gg[1, :, cols], gw_ref[1, h], across, preferred_element_type=f32)
        for g in range(2):
            gwg_ref[g, h] += lax.dot_general(
                low[:, cols], gg[g, :, cols], down, preferred_element_type=f32
            )
    direct[0:tokens, 2 * head :] += lax.dot_general(
        gg[0, :, 2 * head :], gs_ref[0], across, preferred_element_type=f32
    ) + lax.dot_general(gg[1, :, 2 * head :], gs_ref[1], across, preferred_element_type=f32)
    for g in range(2):
        gsg_ref[g] += lax.dot_general(
            low[:, 2 * head :], gg[g, :, 2 * head :], down, preferred_element_type=f32
        )

    def deconvolve(index, sums):
        start = pl.multiple_of(index * 16, 16)
        window = direct[pl.ds(start, 24), :]
        inputs = padded[pl.ds(start, 24), :]
        grad = window[:16]
        out = cw_ref[0:1] * grad
        fold = lambda old, new: old + new[:8] + new[8:]
        new = [fold(sums[0], grad), fold(sums[1], grad * inputs[8:])]
        for k in range(1, taps):
            out = out + cw_ref[k : k + 1] * pltpu.roll(window, 24 - k, 0)[:16]
            new.append(fold(sums[k + 1], grad * pltpu.roll(inputs, k, 0)[8:]))
        gu_ref[0, pl.ds(start, 16), :] = out.astype(bf16)

        @pl.when(index == tokens // 16 - 1)
        def _():
            tail_ref[0] = out[8:]

        return tuple(new)

    zero = jnp.zeros((8, wide), f32)
    sums = lax.fori_loop(0, tokens // 16, deconvolve, (zero,) * (taps + 1))
    for position, value in enumerate(sums):
        taps_ref[position : position + 1] += jnp.sum(value, axis=0, keepdims=True)
    first = direct[0:8, :]
    row = rows_of((8, wide))
    owed = jnp.zeros((8, wide), f32)
    for k in range(1, taps):
        moved = pltpu.roll(first, 8 - k, 0)
        owed = owed + cw_ref[k : k + 1] * jnp.where(row >= 8 - k, moved, 0.0)
    lead_ref[0] = owed


def mlp_kernel(normed_ref, weight_ref, grad_ref, hidden_ref, out_ref):
    part = hidden_ref.shape[1]
    rows = 256

    def step(index, none):
        span = pl.ds(pl.multiple_of(index * rows, rows), rows)
        both = jnp.dot(normed_ref[span, :], weight_ref[...], preferred_element_type=f32)
        act, slope = gelu_both(both[:, :part])
        up = both[:, part:]
        grad = grad_ref[span, :].astype(f32)
        hidden_ref[span, :] = (act * up).astype(bf16)
        out_ref[span, :part] = (grad * up * slope).astype(bf16)
        out_ref[span, part:] = (grad * act).astype(bf16)
        return none

    lax.fori_loop(0, normed_ref.shape[0] // rows, step, 0)


def params(*semantics):
    return pltpu.CompilerParams(dimension_semantics=semantics, vmem_limit_bytes=VMEM_LIMIT)


def per_seq(*shape):
    return pl.BlockSpec((1, *shape), lambda i: (i,) + (0,) * len(shape))


def whole(*shape):
    return pl.BlockSpec(shape, lambda i: (0,) * len(shape))


SCALAR = pl.BlockSpec(memory_space=pltpu.SMEM)


def cost(elements, operations, moved):
    return pl.CostEstimate(
        flops=elements * operations, bytes_accessed=moved, transcendentals=elements * 6
    )


def shards(
    block_input,
    out_cotangent,
    norm_gain,
    in_weight,
    conv_weight,
    conv_bias,
    gate_weight,
    gate_bias,
    decay_param,
    out_weight,
    mlp_gain,
    mlp_weight,
    down_weight,
):
    _, tokens, model = block_input.shape
    taps, rec = conv_weight.shape
    heads, head = gate_weight.shape[1:3]
    members = lax.axis_size("seq")
    devices = lax.axis_size("group")
    hidden = mlp_weight.shape[1] // 2
    assert members == 4 and heads == 10
    half = head // 2
    own = 2 * head + half
    wide = 3 * head
    mine = lax.axis_index("seq")
    odd = mine % 2

    def first_of(member):
        return 5 * (member // 2) + 3 * (member % 2), 5 * (member // 2) + 2

    first, shared = first_of(mine)

    def widen(value, offset=0):
        return jnp.concatenate(
            [
                lax.dynamic_slice_in_dim(value, offset + first * head, 2 * head, value.ndim - 1),
                lax.dynamic_slice_in_dim(value, offset + shared * head, head, value.ndim - 1),
            ],
            -1,
        )

    def owned(value, offset=0):
        return jnp.concatenate(
            [
                lax.dynamic_slice_in_dim(value, offset + first * head, 2 * head, value.ndim - 1),
                lax.dynamic_slice_in_dim(
                    value, offset + shared * head + odd * half, half, value.ndim - 1
                ),
            ],
            -1,
        )

    in_u = gather_group(widen(in_weight))
    in_y = gather_group(owned(in_weight, rec))
    out_piece = model // members
    out_cols = gather_group(
        lax.dynamic_slice_in_dim(out_weight, mine * out_piece, out_piece, 1)
    )
    fine = hidden // devices // members
    down_rows = gather_group(lax.dynamic_slice_in_dim(down_weight, mine * fine, fine, 0))
    part = min(384, hidden // members)
    per_part = part // fine
    parts = hidden // members // part
    cut = mlp_weight.reshape(-1, 2, parts, per_part, members, fine)
    cut = lax.dynamic_index_in_dim(cut, mine, 4, keepdims=False)
    mlp_cols = gather_group(cut.transpose(0, 2, 1, 3, 4).reshape(mlp_weight.shape[0], -1))

    x_own = block_input[0]
    c_own = out_cotangent[0]
    x_all = jnp.concatenate(gather_seq(x_own), 0)
    c_all = jnp.concatenate(gather_seq(c_own), 0)
    normed = rms_low(x_all.astype(f32), norm_gain)

    def rows_for(value, k):
        start, common = first_of(mine ^ k)
        return jnp.concatenate(
            [
                lax.dynamic_slice_in_dim(value, start * head, 2 * head, 0),
                lax.dynamic_slice_in_dim(
                    value, common * head + ((mine ^ k) % 2) * half, half, 0
                ),
            ],
            0,
        )

    out_rows = jnp.zeros((own, model), bf16)
    for k in range(members):
        piece = rows_for(out_cols, k)
        if k:
            piece = swap(piece, k)
        out_rows = lax.dynamic_update_slice_in_dim(out_rows, piece, (mine ^ k) * out_piece, 1)

    u = jnp.dot(normed, in_u, preferred_element_type=f32).reshape(members, tokens, wide)
    y = jnp.dot(normed, in_y, preferred_element_type=f32).reshape(members, tokens, own)
    lead = taps - 1
    rim = jnp.pad(shift(u[:, tokens - lead :], 1), ((0, 0), (8 - lead, 0), (0, 0)))
    odd_flag = odd.astype(jnp.int32).reshape(1)
    cw = widen(conv_weight)
    cb = widen(conv_bias)[None]
    gb = owned(gate_bias)
    soft = -8.0 * owned(jax.nn.softplus(decay_param))[None]
    gw = lax.dynamic_slice_in_dim(gate_weight, first, 2, 1)
    gs = lax.dynamic_slice(
        gate_weight, (0, shared, 0, odd * half), (2, 1, head, half)
    )[:, 0]
    rows = members * tokens
    full = jax.ShapeDtypeStruct((members, tokens, own), f32)
    conv, recur, gate, decay, state_local, decay_cum = pl.pallas_call(
        functools.partial(forward_kernel, head),
        grid=(members,),
        in_specs=[
            SCALAR,
            per_seq(tokens, wide),
            per_seq(8, wide),
            whole(taps, wide),
            whole(1, wide),
            whole(2, 2, head, head),
            whole(2, head, half),
            whole(2, own),
            whole(1, own),
        ],
        out_specs=[per_seq(tokens, wide)] + [per_seq(tokens, own)] * 5,
        out_shape=[jax.ShapeDtypeStruct((members, tokens, wide), f32)] + [full] * 5,
        scratch_shapes=[
            pltpu.VMEM((tokens + 8, wide), f32),
            pltpu.VMEM((tokens, wide), bf16),
            pltpu.VMEM((2, tokens, own), f32),
        ],
        compiler_params=params("arbitrary"),
        cost_estimate=cost(rows * own, 1100, rows * own * 28),
        name="recurrence_forward",
    )(odd_flag, u, rim, cw, cb, gw, gs, gb, soft)
    carried = entering(decay_cum[:, -1], state_local[:, -1], 1)
    carried8 = jnp.broadcast_to(carried[:, None], (members, 8, own))
    h, merged = pl.pallas_call(
        merge_kernel,
        grid=(members,),
        in_specs=[per_seq(tokens, own)] * 2 + [per_seq(8, own), per_seq(tokens, own)],
        out_specs=[per_seq(tokens, own)] * 2,
        out_shape=[full, jax.ShapeDtypeStruct((members, tokens, own), bf16)],
        compiler_params=params("arbitrary"),
        cost_estimate=cost(rows * own, 20, rows * own * 18),
        name="recurrence_merge",
    )(state_local, decay_cum, carried8, y)
    partial = [None] * members
    for k in (3, 1, 2, 0):
        partial[k] = jnp.dot(merged[k], out_rows, preferred_element_type=f32).astype(bf16)
    x32 = x_own.astype(f32)
    resid = x32 + scatter_seq(partial)
    normed2 = jnp.concatenate(gather_seq(rms_low(resid, mlp_gain)), 0)

    grad_hidden = lax.dot_general(
        c_all, down_rows, (((1,), (1,)), ((), ())), preferred_element_type=f32
    )
    width = parts * part
    hidden_low, grad_gu = pl.pallas_call(
        mlp_kernel,
        grid=(parts,),
        in_specs=[
            whole(rows, model),
            pl.BlockSpec((model, 2 * part), lambda i: (0, i)),
            pl.BlockSpec((rows, part), lambda i: (0, i)),
        ],
        out_specs=[
            pl.BlockSpec((rows, part), lambda i: (0, i)),
            pl.BlockSpec((rows, 2 * part), lambda i: (0, i)),
        ],
        out_shape=[
            jax.ShapeDtypeStruct((rows, width), bf16),
            jax.ShapeDtypeStruct((rows, 2 * width), bf16),
        ],
        compiler_params=params("arbitrary"),
        cost_estimate=pl.CostEstimate(
            flops=4 * rows * model * width,
            bytes_accessed=rows * model * 2 + model * width * 4 + rows * width * 10,
            transcendentals=rows * width,
        ),
        name="mlp",
    )(normed2, mlp_cols, grad_hidden)
    partial = [None] * members
    for k in (3, 1, 2, 0):
        partial[k] = lax.dot_general(
            grad_gu[k * tokens : (k + 1) * tokens],
            mlp_cols,
            (((1,), (1,)), ((), ())),
            preferred_element_type=f32,
        ).astype(bf16)
    grad_normed2 = scatter_seq(partial)
    grad_resid_norm, mlp_gain_grad = rms_back(resid, mlp_gain, grad_normed2)
    grad_resid = c_own.astype(f32) + grad_resid_norm
    grad_resid_all = jnp.concatenate(gather_seq(grad_resid.astype(bf16)), 0)

    down = (((0,), (0,)), ((), ()))
    down_sum = scatter_group(
        lax.dot_general(hidden_low, c_all, down, preferred_element_type=f32).astype(bf16)
    )
    mlp_sum = scatter_group(
        lax.dot_general(normed2, grad_gu, down, preferred_element_type=f32).astype(bf16)
    )
    partial = [None] * members
    for k in (3, 1, 2, 0):
        partial[k] = jnp.dot(
            hidden_low[k * tokens : (k + 1) * tokens], down_rows, preferred_element_type=f32
        ).astype(bf16)
    block_out = (resid + scatter_seq(partial)).astype(bf16)[None]

    grad_merged = lax.dot_general(
        grad_resid_all, out_rows, (((1,), (1,)), ((), ())), preferred_element_type=f32
    ).reshape(members, tokens, own)
    grad_h, grad_y, back_local, back_cum = pl.pallas_call(
        adjoint_kernel,
        grid=(members,),
        in_specs=[per_seq(tokens, own)] * 4,
        out_specs=[per_seq(tokens, own)] * 4,
        out_shape=[full, jax.ShapeDtypeStruct((members, tokens, own), bf16), full, full],
        compiler_params=params("arbitrary"),
        cost_estimate=cost(rows * own, 50, rows * own * 30),
        name="recurrence_adjoint",
    )(grad_merged, h, y, decay)
    incoming = entering(back_cum[:, 0], back_local[:, 0], -1)
    incoming8 = jnp.broadcast_to(incoming[:, None], (members, 8, own))
    grad_u, tail, owed, small, tap_sums, gw_grad, gs_grad = pl.pallas_call(
        functools.partial(backward_kernel, head),
        grid=(members,),
        in_specs=[
            SCALAR,
            *[per_seq(tokens, own)] * 4,
            per_seq(8, own),
            per_seq(8, own),
            *[per_seq(tokens, own)] * 3,
            *[per_seq(tokens, wide)] * 2,
            per_seq(8, wide),
            whole(taps, wide),
            whole(2, 2, head, head),
            whole(2, head, half),
            whole(1, own),
        ],
        out_specs=[
            per_seq(tokens, wide),
            per_seq(8, wide),
            per_seq(8, wide),
            whole(8, own),
            whole(8, wide),
            whole(2, 2, head, head),
            whole(2, head, half),
        ],
        out_shape=[
            jax.ShapeDtypeStruct((members, tokens, wide), bf16),
            jax.ShapeDtypeStruct((members, 8, wide), f32),
            jax.ShapeDtypeStruct((members, 8, wide), f32),
            jax.ShapeDtypeStruct((8, own), f32),
            jax.ShapeDtypeStruct((8, wide), f32),
            jax.ShapeDtypeStruct((2, 2, head, head), f32),
            jax.ShapeDtypeStruct((2, head, half), f32),
        ],
        scratch_shapes=[
            pltpu.VMEM((tokens + 8, wide), f32),
            pltpu.VMEM((tokens + 8, own), f32),
            pltpu.VMEM((tokens + 8, own), f32),
            pltpu.VMEM((tokens, wide), bf16),
            pltpu.VMEM((2, tokens, own), bf16),
            pltpu.VMEM((tokens + 8, wide), f32),
        ],
        compiler_params=params("arbitrary"),
        cost_estimate=cost(rows * own, 2200, rows * own * 36),
        name="recurrence_backward",
    )(
        odd_flag, back_local, back_cum, grad_h, h, carried8, incoming8, recur, gate,
        decay, conv, u, rim, cw, gw, gs, soft,
    )
    tail = (tail + shift(owed, -1)).astype(bf16)
    grad_u = lax.dynamic_update_slice(grad_u, tail, (0, tokens - 8, 0))
    flat_u = grad_u.reshape(rows, wide)
    flat_y = grad_y.reshape(rows, own)
    partial = [None] * members
    across = (((1,), (1,)), ((), ()))
    for k in (3, 1, 2, 0):
        partial[k] = (
            lax.dot_general(grad_u[k], in_u, across, preferred_element_type=f32)
            + lax.dot_general(grad_y[k], in_y, across, preferred_element_type=f32)
        ).astype(bf16)
    grad_normed = scatter_seq(partial)
    grad_input_norm, norm_gain_grad = rms_back(x32, norm_gain, grad_normed)
    input_grad = (grad_resid + grad_input_norm)[None]

    y_sum = scatter_group(
        lax.dot_general(normed, flat_y, down, preferred_element_type=f32).astype(bf16)
    )
    u_sum = scatter_group(
        lax.dot_general(normed, flat_u, down, preferred_element_type=f32).astype(bf16)
    )
    out_part = lax.dot_general(
        merged.reshape(rows, own), grad_resid_all, down, preferred_element_type=f32
    ).astype(bf16)
    out_terms = jnp.zeros((rec, out_piece), bf16)
    for k in range(members):
        piece = lax.dynamic_slice_in_dim(out_part, (mine ^ k) * out_piece, out_piece, 1)
        if k:
            piece = swap(piece, k)
        start, common = first_of(mine ^ k)
        out_terms = lax.dynamic_update_slice_in_dim(
            out_terms, piece[: 2 * head], start * head, 0
        )
        out_terms = lax.dynamic_update_slice_in_dim(
            out_terms, piece[2 * head :], common * head + ((mine ^ k) % 2) * half, 0
        )
    out_sum = scatter_group(out_terms)

    down_parts = jnp.stack(gather_seq(down_sum))
    down_grad = jnp.concatenate(
        [lax.dynamic_index_in_dim(down_parts, mine ^ a, 0, keepdims=False) for a in range(members)],
        0,
    ).astype(f32)
    mlp_parts = jnp.stack(gather_seq(mlp_sum))
    mlp_grad = jnp.stack(
        [
            lax.dynamic_index_in_dim(mlp_parts, mine ^ a, 0, keepdims=False).reshape(
                -1, parts, 2, per_part, fine
            )
            for a in range(members)
        ],
        4,
    )
    mlp_grad = mlp_grad.transpose(0, 2, 1, 3, 4, 5).reshape(-1, 2 * hidden).astype(f32)
    out_parts = jnp.stack(gather_seq(out_sum))
    out_grad = jnp.concatenate(
        [lax.dynamic_index_in_dim(out_parts, mine ^ a, 0, keepdims=False) for a in range(members)],
        1,
    ).astype(f32)
    u_parts = gather_seq(u_sum)
    y_parts = gather_seq(y_sum)
    in_grad = jnp.zeros((u_sum.shape[0], 2 * rec), f32)
    for k in range(members):
        start, common = first_of(mine ^ k)
        in_grad = lax.dynamic_update_slice_in_dim(
            in_grad, u_parts[k][:, : 2 * head].astype(f32), start * head, 1
        )
        in_grad = lax.dynamic_update_slice_in_dim(
            in_grad, y_parts[k][:, : 2 * head].astype(f32), rec + start * head, 1
        )
        in_grad = lax.dynamic_update_slice_in_dim(
            in_grad,
            y_parts[k][:, 2 * head :].astype(f32),
            rec + common * head + ((mine ^ k) % 2) * half,
            1,
        )
        if k % 2 == 0:
            both = u_parts[k][:, 2 * head :].astype(f32) + u_parts[k + 1][:, 2 * head :].astype(f32)
            in_grad = lax.dynamic_update_slice_in_dim(in_grad, both, common * head, 1)

    gate_terms = jnp.concatenate([gw_grad[:, 0], gw_grad[:, 1], gs_grad], -1).astype(bf16)
    gate_sum = lax.psum(gate_terms, "group")
    gate_parts = gather_seq(gate_sum.reshape(2 * head, own))
    gate_grad = jnp.zeros((2, heads, head, head), f32)
    for k in range(members):
        start, common = first_of(mine ^ k)
        block = gate_parts[k].reshape(2, head, own).astype(f32)
        pair = block[:, :, : 2 * head].reshape(2, head, 2, head).transpose(0, 2, 1, 3)
        gate_grad = lax.dynamic_update_slice_in_dim(gate_grad, pair, start, 1)
        if k % 2 == 0:
            other = gate_parts[k + 1].reshape(2, head, own).astype(f32)
            halves = jnp.where(
                odd == 1,
                jnp.concatenate([other[..., 2 * head :], block[..., 2 * head :]], -1),
                jnp.concatenate([block[..., 2 * head :], other[..., 2 * head :]], -1),
            )
            gate_grad = lax.dynamic_update_slice_in_dim(gate_grad, halves[:, None], common, 1)

    def place(value, wide_shared):
        out = jnp.zeros((value.shape[0], rec), f32)
        out = lax.dynamic_update_slice_in_dim(out, value[:, : 2 * head], first * head, 1)
        at = shared * head if wide_shared else shared * head + odd * half
        return lax.dynamic_update_slice_in_dim(out, value[:, 2 * head :], at, 1)

    decay_terms = small[2:3] * (-8.0) * owned(jax.nn.sigmoid(decay_param))[None]
    channel = jnp.concatenate(
        [place(tap_sums[: taps + 1], True), place(jnp.concatenate([small[:2], decay_terms], 0), False)],
        0,
    )
    packed = jnp.concatenate([channel.reshape(-1, 128), mlp_gain_grad.reshape(-1, 128)], 0)
    packed = total(packed)
    channel = packed[: (taps + 4) * rec // 128].reshape(taps + 4, rec)
    mlp_gain_grad = packed[(taps + 4) * rec // 128 :].reshape(-1)
    norm_gain_grad = total(norm_gain_grad.reshape(-1, 128)).reshape(-1)
    return (
        block_out,
        input_grad,
        norm_gain_grad,
        in_grad,
        channel[1 : taps + 1],
        channel[0],
        gate_grad,
        channel[taps + 1 : taps + 3],
        channel[taps + 3],
        out_grad,
        mlp_gain_grad,
        mlp_grad,
        down_grad,
    )


def solution(mesh):
    tokens = P("seq", "group", None)
    rows = P("group", None)
    in_specs = (tokens, tokens, P(), rows, P(), P(), P(), P(), P(), rows, P(), rows, rows)
    out_specs = (tokens, tokens, P(), rows, P(), P(), P(), P(), P(), rows, P(), rows, rows)
    return jax.shard_map(shards, mesh=mesh, in_specs=in_specs, out_specs=out_specs, check_vma=False)
```

```python
import functools

import jax
import jax.numpy as jnp
from jax import lax
from jax.experimental import pallas as pl
from jax.experimental.pallas import tpu as pltpu
from jax.sharding import PartitionSpec as P

epsilon = 1e-06
f32 = jnp.float32
bf16 = jnp.bfloat16
VMEM_LIMIT = 58 * 1024 * 1024


def swap(block, k):
    return lax.ppermute(block, "seq", [(i, i ^ k) for i in range(lax.axis_size("seq"))])


def shift(block, distance):
    devices = range(lax.axis_size("group"))
    return lax.ppermute(
        block, "group", [(i - distance, i) for i in devices if i - distance in devices]
    )


def gather_seq(block, hop=None):
    half = block.shape[0] // 2
    first, second = (swap(block, 1), swap(block, 2)) if hop is None else hop
    third = jnp.concatenate([swap(first[:half], 2), swap(second[half:], 1)], 0)
    return [block, first, second, third]


def first_hop(third):
    half = third.shape[0] // 2
    return swap(third[:half], 1), swap(third[half:], 2)


def scatter_seq(parts, hop=None):
    half = parts[0].shape[0] // 2
    own, first, second, third = parts
    top, bottom = first_hop(third) if hop is None else hop
    first_top = swap(first[:half], 1)
    second_bottom = swap(second[half:], 2)
    second_top = swap((second[:half].astype(f32) + top.astype(f32)).astype(bf16), 2)
    first_bottom = swap((first[half:].astype(f32) + bottom.astype(f32)).astype(bf16), 1)
    return jnp.concatenate(
        [
            own[:half].astype(f32) + first_top.astype(f32) + second_top.astype(f32),
            own[half:].astype(f32) + first_bottom.astype(f32) + second_bottom.astype(f32),
        ],
        0,
    )


def gather_group(block):
    return lax.all_gather(block, "group", axis=0, tiled=True)


def scatter_group(block):
    return lax.psum_scatter(block, "group", scatter_dimension=0, tiled=True)


def after(value, *others):
    return lax.optimization_barrier((value, *others))[0]


def total_group(value):
    count = lax.axis_size("group")
    place = lax.axis_index("group")
    route = lambda step: [(i, i ^ step) for i in range(count)]
    steps = [1 << i for i in range(count.bit_length() - 1)]
    for step in steps:
        half = value.shape[0] // 2
        bit = (place // step) % 2
        kept = lax.dynamic_slice_in_dim(value, bit * half, half, 0)
        given = lax.dynamic_slice_in_dim(value, (1 - bit) * half, half, 0)
        got = lax.ppermute(given, "group", route(step))
        value = (kept.astype(f32) + got.astype(f32)).astype(value.dtype)
    for step in reversed(steps):
        bit = (place // step) % 2
        got = lax.ppermute(value, "group", route(step))
        value = jnp.where(
            bit == 0, jnp.concatenate([value, got], 0), jnp.concatenate([got, value], 0)
        )
    return value


def total(value):
    for axis in ("group", "seq"):
        count = lax.axis_size(axis)
        step = 1
        while step < count:
            value = value + lax.ppermute(value, axis, [(i, i ^ step) for i in range(count)])
            step *= 2
    return value


def link(earlier, later):
    return (earlier[0] * later[0], later[1] + later[0] * earlier[1])


def entering(decay, state, sign):
    count = lax.axis_size("group")
    pair = jnp.stack([decay, state])
    near = [shift(pair, sign * distance) for distance in range(1, min(4, count - 1) + 1)]
    decay, state = near[0][0], near[0][1]
    for before in near[1:]:
        decay, state = link((before[0], before[1]), (decay, state))
    covered = len(near)
    while covered < count - 1:
        before = shift(jnp.stack([decay, state]), sign * covered)
        decay, state = link((before[0], before[1]), (decay, state))
        covered *= 2
    return state


def rms_low(value, gain):
    scale = lax.rsqrt(jnp.mean(value * value, axis=-1, keepdims=True) + epsilon)
    return (value * scale * gain).astype(bf16)


def rms_back(value, gain, grad):
    width = value.shape[-1]
    scale = lax.rsqrt(jnp.mean(value * value, axis=-1, keepdims=True) + epsilon)
    scaled = grad * gain
    along = jnp.sum(scaled * value, axis=-1, keepdims=True) / width
    grad_value = scale * scaled - value * (scale * scale * scale * along)
    grad_gain = jnp.sum(grad * value * scale, axis=0)
    return grad_value, grad_gain


ROOT = 0.7978845608028654
CUBE = 0.044715


def gelu(v):
    return 0.5 * v * (1.0 + jnp.tanh(ROOT * (v + CUBE * v * v * v)))


def gelu_both(v):
    square = v * v
    t = jnp.tanh(ROOT * v * (1.0 + CUBE * square))
    half = 0.5 * (1.0 + t)
    slope = half + 0.5 * v * (1.0 - t * t) * (ROOT * (1.0 + 3.0 * CUBE * square))
    return v * half, slope


def one_less_square(double):
    series = jnp.full_like(double, 1.0 / 362880.0)
    for term in (40320.0, 5040.0, 720.0, 120.0, 24.0, 6.0, 2.0, 1.0):
        series = series * double + 1.0 / term
    return -double * series


def rows_of(shape):
    return lax.broadcasted_iota(jnp.int32, shape, 0)


def pick(odd, value, width):
    lanes = value.shape[-1]
    return jnp.where(odd, value[:, lanes - width :], value[:, lanes - 2 * width : lanes - width])


def forward_kernel(
    head, odd_ref, u_ref, rim_ref, cw_ref, cb_ref, gw_ref, gs_ref, gb_ref, sp_ref,
    conv_ref, recur_ref, input_ref, decay_ref, state_ref, cum_ref,
    padded, low, pre,
):
    tokens, wide = u_ref.shape[1:]
    own = recur_ref.shape[2]
    odd = odd_ref[0] == 1
    padded[0:8] = rim_ref[0]
    padded[8:] = u_ref[0]
    taps = cw_ref.shape[0]

    def convolve(index, carry):
        start = pl.multiple_of(index * 32, 32)
        window = padded[pl.ds(start, 40), :]
        out = cb_ref[...] + cw_ref[0:1] * window[8:]
        for k in range(1, taps):
            out = out + cw_ref[k : k + 1] * pltpu.roll(window, k, 0)[8:]
        conv_ref[0, pl.ds(start, 32), :] = out
        low[pl.ds(start, 32), :] = out.astype(bf16)
        return carry

    lax.fori_loop(0, tokens // 32, convolve, 0)
    for g in range(2):
        for h in range(2):
            cols = slice(h * head, (h + 1) * head)
            pre[g, :, cols] = jnp.dot(low[:, cols], gw_ref[g, h], preferred_element_type=f32)
        pre[g, :, 2 * head :] = jnp.dot(low[:, 2 * head :], gs_ref[g], preferred_element_type=f32)
    row = rows_of((8, own))

    def scan(index, carry):
        cum, state = carry
        start = pl.multiple_of(index * 16, 16)
        span = pl.ds(start, 16)
        recur = jax.nn.sigmoid(pre[0, span, :] + gb_ref[0:1])
        gate = jax.nn.sigmoid(pre[1, span, :] + gb_ref[1:2])
        log_decay = recur * sp_ref[...]
        decay = jnp.exp(log_decay)
        conv = conv_ref[0, span, :]
        conv = jnp.concatenate([conv[:, : 2 * head], pick(odd, conv, head // 2)], 1)
        driven = conv * gate * jnp.sqrt(one_less_square(2.0 * log_decay))
        recur_ref[0, span, :] = recur
        input_ref[0, span, :] = gate
        decay_ref[0, span, :] = decay
        for tile in range(2):
            a = decay[tile * 8 : tile * 8 + 8]
            b = driven[tile * 8 : tile * 8 + 8]
            for d in (1, 2, 4):
                there = row >= d
                before_a = jnp.where(there, pltpu.roll(a, d, 0), 1.0)
                before_b = jnp.where(there, pltpu.roll(b, d, 0), 0.0)
                b = b + a * before_b
                a = a * before_a
            b = b + a * state
            a = a * cum
            place = pl.ds(start + tile * 8, 8)
            state_ref[0, place, :] = b
            cum_ref[0, place, :] = a
            cum, state = a[7:8], b[7:8]
        return cum, state

    lax.fori_loop(
        0, tokens // 16, scan, (jnp.ones((1, own), f32), jnp.zeros((1, own), f32))
    )


def merge_kernel(state_ref, cum_ref, carry_ref, pre_ref, h_ref, merged_ref):
    def step(index, none):
        span = pl.ds(pl.multiple_of(index * 32, 32), 32)
        state = state_ref[0, span, :] + cum_ref[0, span, :] * carry_ref[0, 0:1]
        h_ref[0, span, :] = state
        merged_ref[0, span, :] = (state * gelu(pre_ref[0, span, :])).astype(bf16)
        return none

    lax.fori_loop(0, state_ref.shape[1] // 32, step, 0)


def adjoint_kernel(gm_ref, h_ref, pre_ref, decay_ref, gh_ref, gpre_ref, back_ref, cum_ref):
    tokens, own = gm_ref.shape[1:]
    row = rows_of((8, own))
    count = tokens // 16

    def step(index, carry):
        cum, back = carry
        start = pl.multiple_of((count - 1 - index) * 16, 16)
        span = pl.ds(start, 16)
        grad = gm_ref[0, span, :]
        act, slope = gelu_both(pre_ref[0, span, :])
        gpre_ref[0, span, :] = (grad * h_ref[0, span, :] * slope).astype(bf16)
        grad_h = grad * act
        gh_ref[0, span, :] = grad_h
        decay = decay_ref[0, span, :]
        driven = decay * grad_h
        for tile in (1, 0):
            a = decay[tile * 8 : tile * 8 + 8]
            b = driven[tile * 8 : tile * 8 + 8]
            for d in (1, 2, 4):
                there = row < 8 - d
                after_a = jnp.where(there, pltpu.roll(a, 8 - d, 0), 1.0)
                after_b = jnp.where(there, pltpu.roll(b, 8 - d, 0), 0.0)
                b = b + a * after_b
                a = a * after_a
            b = b + a * back
            a = a * cum
            place = pl.ds(start + tile * 8, 8)
            back_ref[0, place, :] = b
            cum_ref[0, place, :] = a
            cum, back = a[0:1], b[0:1]
        return cum, back

    lax.fori_loop(0, count, step, (jnp.ones((1, own), f32), jnp.zeros((1, own), f32)))


def backward_kernel(
    head, odd_ref, back_ref, cum_ref, gh_ref, h_ref, carry_ref, enter_ref, recur_ref, input_ref,
    decay_ref, conv_ref, u_ref, gy_ref, rim_ref, cw_ref, gw_ref, gs_ref, sp_ref,
    gu_ref, tail_ref, lead_ref, small_ref, taps_ref, gwg_ref, gsg_ref,
    padded, ahead, behind, low, gg, direct,
):
    tokens, wide = u_ref.shape[1:]
    own = recur_ref.shape[2]
    half = head // 2
    odd = odd_ref[0] == 1
    taps = cw_ref.shape[0]

    @pl.when(pl.program_id(0) == 0)
    def _():
        small_ref[...] = jnp.zeros_like(small_ref)
        taps_ref[...] = jnp.zeros_like(taps_ref)
        gwg_ref[...] = jnp.zeros_like(gwg_ref)
        gsg_ref[...] = jnp.zeros_like(gsg_ref)

    padded[0:8] = rim_ref[0]
    padded[8:] = u_ref[0]
    behind[0:8] = carry_ref[0]
    ahead[tokens:] = enter_ref[0]
    direct[tokens:] = jnp.zeros((8, wide), f32)
    enter = enter_ref[0, 0:1]

    def prepare(index, none):
        start = pl.multiple_of(index * 32, 32)
        span = pl.ds(start, 32)
        ahead[span, :] = back_ref[0, span, :] + cum_ref[0, span, :] * enter
        behind[pl.ds(start + 8, 32), :] = h_ref[0, span, :]
        return none

    lax.fori_loop(0, tokens // 32, prepare, 0)

    def gates(index, sums):
        sum_recur, sum_input, sum_decay = sums
        start = pl.multiple_of(index * 16, 16)
        span = pl.ds(start, 16)
        after = pltpu.roll(ahead[pl.ds(start, 24), :], 23, 0)[:16]
        before = pltpu.roll(behind[pl.ds(start, 24), :], 1, 0)[8:]
        adj = gh_ref[0, span, :] + after
        recur = recur_ref[0, span, :]
        gate = input_ref[0, span, :]
        decay = decay_ref[0, span, :]
        whole = conv_ref[0, span, :]
        low[span, :] = whole.astype(bf16)
        conv = jnp.concatenate([whole[:, : 2 * head], pick(odd, whole, half)], 1)
        square = one_less_square(2.0 * (recur * sp_ref[...]))
        inverse = lax.rsqrt(square)
        root = square * inverse
        grad_a = adj * before
        part = adj * gate
        grad_direct = part * root
        grad_gate = adj * conv * root
        grad_root = part * conv
        grad_log = decay * (grad_a - grad_root * decay * inverse)
        scaled = grad_log * recur
        grad_recur = scaled * sp_ref[...] * (1.0 - recur)
        grad_input = grad_gate * gate * (1.0 - gate)
        gg[0, span, :] = grad_recur.astype(bf16)
        gg[1, span, :] = grad_input.astype(bf16)
        shared = grad_direct[:, 2 * head :]
        none = jnp.zeros_like(shared)
        direct[span, :] = jnp.concatenate(
            [grad_direct[:, : 2 * head], jnp.where(odd, none, shared), jnp.where(odd, shared, none)],
            1,
        )
        fold = lambda old, new: old + new[:8] + new[8:]
        return fold(sum_recur, grad_recur), fold(sum_input, grad_input), fold(sum_decay, scaled)

    zero = jnp.zeros((8, own), f32)
    sums = lax.fori_loop(0, tokens // 16, gates, (zero, zero, zero))
    for position, value in enumerate(sums):
        small_ref[position : position + 1] += jnp.sum(value, axis=0, keepdims=True)
    across = (((1,), (1,)), ((), ()))
    down = (((0,), (0,)), ((), ()))
    for h in range(2):
        cols = slice(h * head, (h + 1) * head)
        direct[0:tokens, cols] += lax.dot_general(
            gg[0, :, cols], gw_ref[0, h], across, preferred_element_type=f32
        ) + lax.dot_general(gg[1, :, cols], gw_ref[1, h], across, preferred_element_type=f32)
        for g in range(2):
            gwg_ref[g, h] += lax.dot_general(
                low[:, cols], gg[g, :, cols], down, preferred_element_type=f32
            )
    direct[0:tokens, 2 * head :] += lax.dot_general(
        gg[0, :, 2 * head :], gs_ref[0], across, preferred_element_type=f32
    ) + lax.dot_general(gg[1, :, 2 * head :], gs_ref[1], across, preferred_element_type=f32)
    for g in range(2):
        gsg_ref[g] += lax.dot_general(
            low[:, 2 * head :], gg[g, :, 2 * head :], down, preferred_element_type=f32
        )

    def deconvolve(index, sums):
        start = pl.multiple_of(index * 16, 16)
        window = direct[pl.ds(start, 24), :]
        inputs = padded[pl.ds(start, 24), :]
        grad = window[:16]
        out = cw_ref[0:1] * grad
        fold = lambda old, new: old + new[:8] + new[8:]
        new = [fold(sums[0], grad), fold(sums[1], grad * inputs[8:])]
        for k in range(1, taps):
            out = out + cw_ref[k : k + 1] * pltpu.roll(window, 24 - k, 0)[:16]
            new.append(fold(sums[k + 1], grad * pltpu.roll(inputs, k, 0)[8:]))
        gu_ref[0, pl.ds(start, 16), :wide] = out.astype(bf16)
        gu_ref[0, pl.ds(start, 16), wide:] = gy_ref[0, pl.ds(start, 16), :]

        @pl.when(index == tokens // 16 - 1)
        def _():
            tail_ref[0] = out[8:]

        return tuple(new)

    zero = jnp.zeros((8, wide), f32)
    sums = lax.fori_loop(0, tokens // 16, deconvolve, (zero,) * (taps + 1))
    for position, value in enumerate(sums):
        taps_ref[position : position + 1] += jnp.sum(value, axis=0, keepdims=True)
    first = direct[0:8, :]
    row = rows_of((8, wide))
    owed = jnp.zeros((8, wide), f32)
    for k in range(1, taps):
        moved = pltpu.roll(first, 8 - k, 0)
        owed = owed + cw_ref[k : k + 1] * jnp.where(row >= 8 - k, moved, 0.0)
    lead_ref[0] = owed


def mlp_kernel(normed_ref, weight_ref, grad_ref, hidden_ref, out_ref):
    part = hidden_ref.shape[1]
    rows = 512

    def step(index, none):
        span = pl.ds(pl.multiple_of(index * rows, rows), rows)
        both = jnp.dot(normed_ref[span, :], weight_ref[...], preferred_element_type=f32)
        act, slope = gelu_both(both[:, :part])
        up = both[:, part:]
        grad = grad_ref[span, :].astype(f32)
        hidden_ref[span, :] = (act * up).astype(bf16)
        out_ref[span, :part] = (grad * up * slope).astype(bf16)
        out_ref[span, part:] = (grad * act).astype(bf16)
        return none

    lax.fori_loop(0, normed_ref.shape[0] // rows, step, 0)


def spread_mlp_kernel(layout, mine_ref, a_ref, b_ref, c_ref, d_ref, out_ref):
    parts, per_part, fine = layout
    blocks = (a_ref, b_ref, c_ref, d_ref)
    part = per_part * fine
    span = part * len(blocks)
    for mine in range(len(blocks)):

        @pl.when(mine_ref[0] == mine)
        def _(mine=mine):
            for p in range(parts):
                for h in range(2):
                    base = (2 * p + h) * part
                    wholes = [blocks[k][:, base : base + part].astype(f32) for k in range(len(blocks))]
                    pieces = [
                        wholes[mine ^ a][:, g * fine : (g + 1) * fine]
                        for g in range(per_part)
                        for a in range(len(blocks))
                    ]
                    at = (h * parts + p) * span
                    out_ref[:, at : at + span] = jnp.concatenate(pieces, 1)


def spread_in_kernel(head, mine_ref, a_ref, b_ref, c_ref, d_ref, out_ref):
    blocks = (a_ref, b_ref, c_ref, d_ref)
    half = head // 2
    wide = 3 * head
    rec = out_ref.shape[1] // 2
    for mine in range(len(blocks)):

        @pl.when(mine_ref[0] == mine)
        def _(mine=mine):
            for k, block in enumerate(blocks):
                member = mine ^ k
                first, shared = 5 * (member // 2) + 3 * (member % 2), 5 * (member // 2) + 2
                at = first * head
                out_ref[:, at : at + 2 * head] = block[:, : 2 * head].astype(f32)
                out_ref[:, rec + at : rec + at + 2 * head] = block[:, wide : wide + 2 * head].astype(f32)
                at = rec + shared * head + (member % 2) * half
                out_ref[:, at : at + half] = block[:, wide + 2 * head :].astype(f32)
                if k % 2 == 0:
                    at = shared * head
                    out_ref[:, at : at + head] = block[:, 2 * head : wide].astype(f32) + blocks[k + 1][
                        :, 2 * head : wide
                    ].astype(f32)


def spread(kernel, mine, blocks, columns, name):
    rows, wide = blocks[0].shape
    step = min(32, rows)
    piece = pl.BlockSpec((step, wide), lambda i: (i, 0))
    return pl.pallas_call(
        kernel,
        grid=(rows // step,),
        in_specs=[SCALAR] + [piece] * len(blocks),
        out_specs=pl.BlockSpec((step, columns), lambda i: (i, 0)),
        out_shape=jax.ShapeDtypeStruct((rows, columns), f32),
        compiler_params=params("arbitrary"),
        cost_estimate=cost(8),
        name=name,
    )(mine.astype(jnp.int32).reshape(1), *blocks)


def params(*semantics):
    return pltpu.CompilerParams(dimension_semantics=semantics, vmem_limit_bytes=VMEM_LIMIT)


def per_seq(*shape):
    return pl.BlockSpec((1, *shape), lambda i: (i,) + (0,) * len(shape))


def whole(*shape):
    return pl.BlockSpec(shape, lambda i: (0,) * len(shape))


SCALAR = pl.BlockSpec(memory_space=pltpu.SMEM)


def cost(microseconds):
    return pl.CostEstimate(
        flops=int(microseconds * 1e9), bytes_accessed=int(microseconds * 3e6), transcendentals=0
    )


def shards(
    block_input,
    out_cotangent,
    norm_gain,
    in_weight,
    conv_weight,
    conv_bias,
    gate_weight,
    gate_bias,
    decay_param,
    out_weight,
    mlp_gain,
    mlp_weight,
    down_weight,
):
    _, tokens, model = block_input.shape
    taps, rec = conv_weight.shape
    heads, head = gate_weight.shape[1:3]
    members = lax.axis_size("seq")
    devices = lax.axis_size("group")
    hidden = mlp_weight.shape[1] // 2
    assert members == 4 and heads == 10
    half = head // 2
    own = 2 * head + half
    wide = 3 * head
    mine = lax.axis_index("seq")
    odd = mine % 2

    def first_of(member):
        return 5 * (member // 2) + 3 * (member % 2), 5 * (member // 2) + 2

    first, shared = first_of(mine)

    def widen(value, offset=0):
        return jnp.concatenate(
            [
                lax.dynamic_slice_in_dim(value, offset + first * head, 2 * head, value.ndim - 1),
                lax.dynamic_slice_in_dim(value, offset + shared * head, head, value.ndim - 1),
            ],
            -1,
        )

    def owned(value, offset=0):
        return jnp.concatenate(
            [
                lax.dynamic_slice_in_dim(value, offset + first * head, 2 * head, value.ndim - 1),
                lax.dynamic_slice_in_dim(
                    value, offset + shared * head + odd * half, half, value.ndim - 1
                ),
            ],
            -1,
        )

    in_cols = gather_group(jnp.concatenate([widen(in_weight), owned(in_weight, rec)], 1))
    in_u, in_y = in_cols[:, :wide], in_cols[:, wide:]
    x_own = block_input[0]
    x_blocks = gather_seq(x_own)
    x_all = jnp.concatenate(x_blocks, 0)
    c_own = after(out_cotangent[0], x_blocks[1])
    c_blocks = gather_seq(c_own)
    c_all = jnp.concatenate(c_blocks, 0)
    fine = hidden // devices // members
    part = min(384, hidden // members)
    per_part = part // fine
    parts = hidden // members // part
    cut = after(mlp_weight, x_blocks[1]).reshape(-1, 2, parts, per_part, members, fine)
    cut = lax.dynamic_index_in_dim(cut, mine, 4, keepdims=False)
    cut = cut.transpose(0, 2, 1, 3, 4).reshape(mlp_weight.shape[0], -1)
    normed = after(rms_low(x_all.astype(f32), norm_gain), cut)
    out_piece = model // members
    out_cols = gather_group(
        after(lax.dynamic_slice_in_dim(out_weight, mine * out_piece, out_piece, 1), in_cols, normed)
    )
    def rows_for(value, k):
        start, common = first_of(mine ^ k)
        return jnp.concatenate(
            [
                lax.dynamic_slice_in_dim(value, start * head, 2 * head, 0),
                lax.dynamic_slice_in_dim(
                    value, common * head + ((mine ^ k) % 2) * half, half, 0
                ),
            ],
            0,
        )

    out_rows = jnp.zeros((own, model), bf16)
    for k in range(members):
        piece = rows_for(out_cols, k)
        if k:
            piece = swap(piece, k)
        out_rows = lax.dynamic_update_slice_in_dim(out_rows, piece, (mine ^ k) * out_piece, 1)

    u = jnp.dot(normed, in_u, preferred_element_type=f32).reshape(members, tokens, wide)
    u = after(u, c_blocks[1], c_blocks[2])
    y = jnp.dot(normed, in_y, preferred_element_type=f32).reshape(members, tokens, own)
    lead = taps - 1
    rim = jnp.pad(shift(u[:, tokens - lead :], 1), ((0, 0), (8 - lead, 0), (0, 0)))
    odd_flag = odd.astype(jnp.int32).reshape(1)
    cw = widen(conv_weight)
    cb = widen(conv_bias)[None]
    gb = owned(gate_bias)
    soft = -8.0 * owned(jax.nn.softplus(decay_param))[None]
    gw = lax.dynamic_slice_in_dim(gate_weight, first, 2, 1)
    gs = lax.dynamic_slice(
        gate_weight, (0, shared, 0, odd * half), (2, 1, head, half)
    )[:, 0]
    rows = members * tokens
    full = jax.ShapeDtypeStruct((members, tokens, own), f32)
    conv, recur, gate, decay, state_local, decay_cum = pl.pallas_call(
        functools.partial(forward_kernel, head),
        grid=(members,),
        in_specs=[
            SCALAR,
            per_seq(tokens, wide),
            per_seq(8, wide),
            whole(taps, wide),
            whole(1, wide),
            whole(2, 2, head, head),
            whole(2, head, half),
            whole(2, own),
            whole(1, own),
        ],
        out_specs=[per_seq(tokens, wide)] + [per_seq(tokens, own)] * 5,
        out_shape=[jax.ShapeDtypeStruct((members, tokens, wide), f32)] + [full] * 5,
        scratch_shapes=[
            pltpu.VMEM((tokens + 8, wide), f32),
            pltpu.VMEM((tokens, wide), bf16),
            pltpu.VMEM((2, tokens, own), f32),
        ],
        compiler_params=params("arbitrary"),
        cost_estimate=cost(14),
        name="recurrence_forward",
    )(odd_flag, u, rim, cw, cb, gw, gs, gb, soft)
    down_rows = gather_group(
        after(
            lax.dynamic_slice_in_dim(down_weight, mine * fine, fine, 0), out_cols, decay_cum
        )
    )
    carried = entering(decay_cum[:, -1], state_local[:, -1], 1)
    carried = after(carried, out_rows)
    carried8 = jnp.broadcast_to(carried[:, None], (members, 8, own))
    h, merged = pl.pallas_call(
        merge_kernel,
        grid=(members,),
        in_specs=[per_seq(tokens, own)] * 2 + [per_seq(8, own), per_seq(tokens, own)],
        out_specs=[per_seq(tokens, own)] * 2,
        out_shape=[full, jax.ShapeDtypeStruct((members, tokens, own), bf16)],
        compiler_params=params("arbitrary"),
        cost_estimate=cost(14),
        name="recurrence_merge",
    )(state_local, decay_cum, carried8, y)
    partial = jnp.dot(merged.reshape(rows, own), out_rows, preferred_element_type=f32)
    partial = partial.astype(bf16)
    mlp_cols = gather_group(after(cut, down_rows, merged))
    partial = lax.optimization_barrier(partial).reshape(members, tokens, model)
    x32 = x_own.astype(f32)
    grad_hidden = lax.dot_general(
        c_all, down_rows, (((1,), (1,)), ((), ())), preferred_element_type=f32
    )
    resid = after(x32 + scatter_seq(partial), grad_hidden)
    normed2 = jnp.concatenate(gather_seq(rms_low(resid, mlp_gain)), 0)

    width = parts * part
    hidden_low, grad_gu = pl.pallas_call(
        mlp_kernel,
        grid=(parts,),
        in_specs=[
            whole(rows, model),
            pl.BlockSpec((model, 2 * part), lambda i: (0, i)),
            pl.BlockSpec((rows, part), lambda i: (0, i)),
        ],
        out_specs=[
            pl.BlockSpec((rows, part), lambda i: (0, i)),
            pl.BlockSpec((rows, 2 * part), lambda i: (0, i)),
        ],
        out_shape=[
            jax.ShapeDtypeStruct((rows, width), bf16),
            jax.ShapeDtypeStruct((rows, 2 * width), bf16),
        ],
        compiler_params=params("arbitrary"),
        cost_estimate=pl.CostEstimate(
            flops=4 * rows * model * width,
            bytes_accessed=rows * model * 2 + model * width * 4 + rows * width * 10,
            transcendentals=rows * width,
        ),
        name="mlp",
    )(normed2, mlp_cols, grad_hidden)
    across = (((1,), (1,)), ((), ()))
    down = (((0,), (0,)), ((), ()))
    down_part = lax.dot_general(hidden_low, c_all, down, preferred_element_type=f32).astype(bf16)
    down_sum = scatter_group(down_part)
    partial = lax.dot_general(
        after(grad_gu, down_part), mlp_cols, across, preferred_element_type=f32
    ).astype(bf16)
    mlp_part = lax.dot_general(
        normed2, after(grad_gu, partial), down, preferred_element_type=f32
    ).astype(bf16)
    grad_normed2 = scatter_seq(lax.optimization_barrier(partial).reshape(members, tokens, model))
    final = jnp.dot(
        after(hidden_low, mlp_part), down_rows, preferred_element_type=f32
    ).astype(bf16)
    grad_normed2 = after(grad_normed2, final)
    grad_resid_norm, mlp_gain_grad = rms_back(resid, mlp_gain, grad_normed2)
    grad_resid = c_own.astype(f32) + grad_resid_norm
    grad_resid_all = jnp.concatenate(gather_seq(grad_resid.astype(bf16)), 0)
    mlp_sum = scatter_group(after(mlp_part, down_sum, grad_normed2))

    final = after(final, grad_resid_all).reshape(members, tokens, model)
    final_hop = first_hop(final[3])
    block_out = (resid + scatter_seq(final, final_hop)).astype(bf16)[None]
    grad_merged = lax.dot_general(
        grad_resid_all, out_rows, (((1,), (1,)), ((), ())), preferred_element_type=f32
    ).reshape(members, tokens, own)
    grad_merged = after(grad_merged, *final_hop)
    down_first = after(down_sum, *final_hop)
    down_hop = swap(down_first, 1), swap(down_first, 2)
    grad_h, grad_y, back_local, back_cum = pl.pallas_call(
        adjoint_kernel,
        grid=(members,),
        in_specs=[per_seq(tokens, own)] * 4,
        out_specs=[per_seq(tokens, own)] * 4,
        out_shape=[full, jax.ShapeDtypeStruct((members, tokens, own), bf16), full, full],
        compiler_params=params("arbitrary"),
        cost_estimate=cost(10),
        name="recurrence_adjoint",
    )(grad_merged, h, y, decay)
    incoming = entering(back_cum[:, 0], back_local[:, 0], -1)
    incoming8 = jnp.broadcast_to(incoming[:, None], (members, 8, own))
    grad_proj, tail, owed, small, tap_sums, gw_grad, gs_grad = pl.pallas_call(
        functools.partial(backward_kernel, head),
        grid=(members,),
        in_specs=[
            SCALAR,
            *[per_seq(tokens, own)] * 4,
            per_seq(8, own),
            per_seq(8, own),
            *[per_seq(tokens, own)] * 3,
            *[per_seq(tokens, wide)] * 2,
            per_seq(tokens, own),
            per_seq(8, wide),
            whole(taps, wide),
            whole(2, 2, head, head),
            whole(2, head, half),
            whole(1, own),
        ],
        out_specs=[
            per_seq(tokens, wide + own),
            per_seq(8, wide),
            per_seq(8, wide),
            whole(8, own),
            whole(8, wide),
            whole(2, 2, head, head),
            whole(2, head, half),
        ],
        out_shape=[
            jax.ShapeDtypeStruct((members, tokens, wide + own), bf16),
            jax.ShapeDtypeStruct((members, 8, wide), f32),
            jax.ShapeDtypeStruct((members, 8, wide), f32),
            jax.ShapeDtypeStruct((8, own), f32),
            jax.ShapeDtypeStruct((8, wide), f32),
            jax.ShapeDtypeStruct((2, 2, head, head), f32),
            jax.ShapeDtypeStruct((2, head, half), f32),
        ],
        scratch_shapes=[
            pltpu.VMEM((tokens + 8, wide), f32),
            pltpu.VMEM((tokens + 8, own), f32),
            pltpu.VMEM((tokens + 8, own), f32),
            pltpu.VMEM((tokens, wide), bf16),
            pltpu.VMEM((2, tokens, own), bf16),
            pltpu.VMEM((tokens + 8, wide), f32),
        ],
        compiler_params=params("arbitrary"),
        cost_estimate=cost(19),
        name="recurrence_backward",
    )(
        odd_flag, back_local, back_cum, grad_h, h, carried8, incoming8, recur, gate,
        decay, conv, u, grad_y, rim, cw, gw, gs, soft,
    )
    tail = (tail + shift(owed, -1)).astype(bf16)
    grad_proj = lax.dynamic_update_slice(grad_proj, tail, (0, tokens - 8, 0))
    grad_proj = grad_proj.reshape(rows, wide + own)
    out_part = lax.dot_general(
        merged.reshape(rows, own), grad_resid_all, down, preferred_element_type=f32
    ).astype(bf16)
    out_terms = jnp.zeros((rec, out_piece), bf16)
    for k in range(members):
        piece = lax.dynamic_slice_in_dim(out_part, (mine ^ k) * out_piece, out_piece, 1)
        if k:
            piece = swap(piece, k)
        start, common = first_of(mine ^ k)
        out_terms = lax.dynamic_update_slice_in_dim(
            out_terms, piece[: 2 * head], start * head, 0
        )
        out_terms = lax.dynamic_update_slice_in_dim(
            out_terms, piece[2 * head :], common * head + ((mine ^ k) % 2) * half, 0
        )
    gate_terms = jnp.concatenate([gw_grad[:, 0], gw_grad[:, 1], gs_grad], -1).reshape(-1, own)
    decay_terms = small[2:3] * (-8.0) * owned(jax.nn.sigmoid(decay_param))[None]
    sizes = ((taps + 1) * wide, 3 * own, model)
    small_terms = jnp.concatenate(
        [
            tap_sums[: taps + 1].reshape(-1),
            small[:2].reshape(-1),
            decay_terms.reshape(-1),
            mlp_gain_grad,
        ]
    )
    small_rows = 64
    small_terms = jnp.pad(small_terms, (0, small_rows * own - small_terms.shape[0]))
    terms = jnp.concatenate([gate_terms, small_terms.reshape(small_rows, own)], 0).astype(bf16)
    group_terms = total_group(terms)
    partial = lax.dot_general(
        after(grad_proj, out_terms, *down_hop, group_terms), in_cols, across, preferred_element_type=f32
    )
    partial = lax.optimization_barrier(partial.astype(bf16)).reshape(members, tokens, model)
    hop = first_hop(partial[3])
    out_sum = scatter_group(after(out_terms, mlp_sum, grad_proj))
    in_part = lax.dot_general(normed, grad_proj, down, preferred_element_type=f32).astype(bf16)
    in_sum = scatter_group(after(in_part, out_sum, *hop))

    out_blocks = gather_seq(out_sum)
    grad_normed = scatter_seq(partial, (after(hop[0], out_sum), after(hop[1], out_sum)))
    mlp_late = after(mlp_sum, out_sum)
    mlp_hop = swap(mlp_late, 1), swap(mlp_late, 2)
    term_parts = gather_seq(after(group_terms, *hop))
    gate_parts = [after(piece[: 2 * head], in_sum) for piece in term_parts]
    small_parts = jnp.stack([piece[2 * head :].reshape(-1) for piece in term_parts])
    grad_input_norm, norm_gain_grad = rms_back(x32, norm_gain, grad_normed)
    input_grad = (grad_resid + grad_input_norm)[None]

    mlp_blocks = gather_seq(mlp_late, mlp_hop)
    mlp_grad = spread(
        functools.partial(spread_mlp_kernel, (parts, per_part, fine)),
        mine,
        mlp_blocks,
        2 * hidden,
        "spread_mlp",
    )
    out_parts = jnp.stack(out_blocks)
    out_grad = jnp.concatenate(
        [lax.dynamic_index_in_dim(out_parts, mine ^ a, 0, keepdims=False) for a in range(members)],
        1,
    ).astype(f32)
    down_parts = jnp.stack(gather_seq(down_sum, down_hop))
    down_grad = jnp.concatenate(
        [lax.dynamic_index_in_dim(down_parts, mine ^ a, 0, keepdims=False) for a in range(members)],
        0,
    ).astype(f32)
    gate_grad = jnp.zeros((2, heads, head, head), f32)
    for k in range(members):
        start, common = first_of(mine ^ k)
        block = gate_parts[k].reshape(2, head, own).astype(f32)
        pair = block[:, :, : 2 * head].reshape(2, head, 2, head).transpose(0, 2, 1, 3)
        gate_grad = lax.dynamic_update_slice_in_dim(gate_grad, pair, start, 1)
        if k % 2 == 0:
            other = gate_parts[k + 1].reshape(2, head, own).astype(f32)
            halves = jnp.where(
                odd == 1,
                jnp.concatenate([other[..., 2 * head :], block[..., 2 * head :]], -1),
                jnp.concatenate([block[..., 2 * head :], other[..., 2 * head :]], -1),
            )
            gate_grad = lax.dynamic_update_slice_in_dim(gate_grad, halves[:, None], common, 1)

    def place(value, member, wide_shared):
        start, common = first_of(member)
        at = common * head if wide_shared else common * head + (member % 2) * half
        out = jnp.zeros((value.shape[0], rec), f32)
        out = lax.dynamic_update_slice_in_dim(out, value[:, : 2 * head], start * head, 1)
        return lax.dynamic_update_slice_in_dim(out, value[:, 2 * head :], at, 1)

    tap_grads, own_grads, mlp_gain_grad = 0.0, 0.0, 0.0
    for member in range(members):
        piece = lax.dynamic_index_in_dim(small_parts, mine ^ member, 0, keepdims=False).astype(f32)
        one, two, three, _ = jnp.split(
            piece, (sizes[0], sizes[0] + sizes[1], sizes[0] + sizes[1] + sizes[2])
        )
        tap_grads = tap_grads + place(one.reshape(-1, wide), member, True)
        own_grads = own_grads + place(two.reshape(-1, own), member, False)
        mlp_gain_grad = mlp_gain_grad + three
    norm_gain_grad = total(norm_gain_grad.reshape(-1, 128)).reshape(-1)
    in_grad = spread(
        functools.partial(spread_in_kernel, head), mine, gather_seq(after(in_sum, *mlp_hop, *out_blocks, *term_parts)), 2 * rec, "spread_in"
    )

    return (
        block_out,
        input_grad,
        norm_gain_grad,
        in_grad,
        tap_grads[1:],
        tap_grads[0],
        gate_grad,
        own_grads[:2],
        own_grads[2],
        out_grad,
        mlp_gain_grad,
        mlp_grad,
        down_grad,
    )


def solution(mesh):
    tokens = P("seq", "group", None)
    rows = P("group", None)
    in_specs = (tokens, tokens, P(), rows, P(), P(), P(), P(), P(), rows, P(), rows, rows)
    out_specs = (tokens, tokens, P(), rows, P(), P(), P(), P(), P(), rows, P(), rows, rows)
    return jax.shard_map(shards, mesh=mesh, in_specs=in_specs, out_specs=out_specs, check_vma=False)
```

```python
import functools

import jax
import jax.numpy as jnp
from jax import lax
from jax.experimental import pallas as pl
from jax.experimental.pallas import tpu as pltpu
from jax.sharding import PartitionSpec as P

epsilon = 1e-06
f32 = jnp.float32
bf16 = jnp.bfloat16
VMEM_LIMIT = 58 * 1024 * 1024


def swap(block, k):
    return lax.ppermute(block, "seq", [(i, i ^ k) for i in range(lax.axis_size("seq"))])


def shift(block, distance):
    devices = range(lax.axis_size("group"))
    return lax.ppermute(
        block, "group", [(i - distance, i) for i in devices if i - distance in devices]
    )


def gather_seq(block, hop=None):
    half = block.shape[0] // 2
    first, second = (swap(block, 1), swap(block, 2)) if hop is None else hop
    third = jnp.concatenate([swap(first[:half], 2), swap(second[half:], 1)], 0)
    return [block, first, second, third]


def first_hop(third):
    half = third.shape[0] // 2
    return swap(third[:half], 1), swap(third[half:], 2)


def scatter_seq(parts, hop=None):
    half = parts[0].shape[0] // 2
    own, first, second, third = parts
    top, bottom = first_hop(third) if hop is None else hop
    first_top = swap(first[:half], 1)
    second_bottom = swap(second[half:], 2)
    second_top = swap((second[:half].astype(f32) + top.astype(f32)).astype(bf16), 2)
    first_bottom = swap((first[half:].astype(f32) + bottom.astype(f32)).astype(bf16), 1)
    return jnp.concatenate(
        [
            own[:half].astype(f32) + first_top.astype(f32) + second_top.astype(f32),
            own[half:].astype(f32) + first_bottom.astype(f32) + second_bottom.astype(f32),
        ],
        0,
    )


def gather_group(block):
    return lax.all_gather(block, "group", axis=0, tiled=True)


def scatter_group(block):
    return lax.psum_scatter(block, "group", scatter_dimension=0, tiled=True)


def after(value, *others):
    return lax.optimization_barrier((value, *others))[0]


def total_group(value):
    count = lax.axis_size("group")
    place = lax.axis_index("group")
    route = lambda step: [(i, i ^ step) for i in range(count)]
    steps = [1 << i for i in range(count.bit_length() - 1)]
    for step in steps:
        half = value.shape[0] // 2
        bit = (place // step) % 2
        kept = lax.dynamic_slice_in_dim(value, bit * half, half, 0)
        given = lax.dynamic_slice_in_dim(value, (1 - bit) * half, half, 0)
        got = lax.ppermute(given, "group", route(step))
        value = (kept.astype(f32) + got.astype(f32)).astype(value.dtype)
    for step in reversed(steps):
        bit = (place // step) % 2
        got = lax.ppermute(value, "group", route(step))
        value = jnp.where(
            bit == 0, jnp.concatenate([value, got], 0), jnp.concatenate([got, value], 0)
        )
    return value


def total(value):
    for axis in ("group", "seq"):
        count = lax.axis_size(axis)
        step = 1
        while step < count:
            value = value + lax.ppermute(value, axis, [(i, i ^ step) for i in range(count)])
            step *= 2
    return value


def link(earlier, later):
    return (earlier[0] * later[0], later[1] + later[0] * earlier[1])


def entering(decay, state, sign):
    count = lax.axis_size("group")
    pair = jnp.stack([decay, state])
    near = [shift(pair, sign * distance) for distance in range(1, min(4, count - 1) + 1)]
    decay, state = near[0][0], near[0][1]
    for before in near[1:]:
        decay, state = link((before[0], before[1]), (decay, state))
    covered = len(near)
    while covered < count - 1:
        before = shift(jnp.stack([decay, state]), sign * covered)
        decay, state = link((before[0], before[1]), (decay, state))
        covered *= 2
    return state


def rms_low(value, gain):
    scale = lax.rsqrt(jnp.mean(value * value, axis=-1, keepdims=True) + epsilon)
    return (value * scale * gain).astype(bf16)


def rms_back(value, gain, grad):
    width = value.shape[-1]
    scale = lax.rsqrt(jnp.mean(value * value, axis=-1, keepdims=True) + epsilon)
    scaled = grad * gain
    along = jnp.sum(scaled * value, axis=-1, keepdims=True) / width
    grad_value = scale * scaled - value * (scale * scale * scale * along)
    grad_gain = jnp.sum(grad * value * scale, axis=0)
    return grad_value, grad_gain


ROOT = 0.7978845608028654
CUBE = 0.044715


def gelu(v):
    return 0.5 * v * (1.0 + jnp.tanh(ROOT * (v + CUBE * v * v * v)))


def gelu_both(v):
    square = v * v
    t = jnp.tanh(ROOT * v * (1.0 + CUBE * square))
    half = 0.5 * (1.0 + t)
    slope = half + 0.5 * v * (1.0 - t * t) * (ROOT * (1.0 + 3.0 * CUBE * square))
    return v * half, slope


def one_less_square(double):
    series = jnp.full_like(double, 1.0 / 362880.0)
    for term in (40320.0, 5040.0, 720.0, 120.0, 24.0, 6.0, 2.0, 1.0):
        series = series * double + 1.0 / term
    return -double * series


def rows_of(shape):
    return lax.broadcasted_iota(jnp.int32, shape, 0)


def pick(odd, value, width):
    lanes = value.shape[-1]
    return jnp.where(odd, value[:, lanes - width :], value[:, lanes - 2 * width : lanes - width])


def forward_kernel(
    head, odd_ref, u_ref, rim_ref, cw_ref, cb_ref, gw_ref, gs_ref, gb_ref, sp_ref,
    conv_ref, recur_ref, input_ref, decay_ref, state_ref, cum_ref,
    padded, low, pre,
):
    tokens, wide = u_ref.shape[1:]
    own = recur_ref.shape[2]
    odd = odd_ref[0] == 1
    padded[0:8] = rim_ref[0]
    padded[8:] = u_ref[0]
    taps = cw_ref.shape[0]

    def convolve(index, carry):
        start = pl.multiple_of(index * 32, 32)
        window = padded[pl.ds(start, 40), :]
        out = cb_ref[...] + cw_ref[0:1] * window[8:]
        for k in range(1, taps):
            out = out + cw_ref[k : k + 1] * pltpu.roll(window, k, 0)[8:]
        conv_ref[0, pl.ds(start, 32), :] = out
        low[pl.ds(start, 32), :] = out.astype(bf16)
        return carry

    lax.fori_loop(0, tokens // 32, convolve, 0)
    for g in range(2):
        for h in range(2):
            cols = slice(h * head, (h + 1) * head)
            pre[g, :, cols] = jnp.dot(low[:, cols], gw_ref[g, h], preferred_element_type=f32)
        pre[g, :, 2 * head :] = jnp.dot(low[:, 2 * head :], gs_ref[g], preferred_element_type=f32)
    row = rows_of((8, own))

    def scan(index, carry):
        cum, state = carry
        start = pl.multiple_of(index * 16, 16)
        span = pl.ds(start, 16)
        recur = jax.nn.sigmoid(pre[0, span, :] + gb_ref[0:1])
        gate = jax.nn.sigmoid(pre[1, span, :] + gb_ref[1:2])
        log_decay = recur * sp_ref[...]
        decay = jnp.exp(log_decay)
        conv = conv_ref[0, span, :]
        conv = jnp.concatenate([conv[:, : 2 * head], pick(odd, conv, head // 2)], 1)
        driven = conv * gate * jnp.sqrt(one_less_square(2.0 * log_decay))
        recur_ref[0, span, :] = recur
        input_ref[0, span, :] = gate
        decay_ref[0, span, :] = decay
        for tile in range(2):
            a = decay[tile * 8 : tile * 8 + 8]
            b = driven[tile * 8 : tile * 8 + 8]
            for d in (1, 2, 4):
                there = row >= d
                before_a = jnp.where(there, pltpu.roll(a, d, 0), 1.0)
                before_b = jnp.where(there, pltpu.roll(b, d, 0), 0.0)
                b = b + a * before_b
                a = a * before_a
            b = b + a * state
            a = a * cum
            place = pl.ds(start + tile * 8, 8)
            state_ref[0, place, :] = b
            cum_ref[0, place, :] = a
            cum, state = a[7:8], b[7:8]
        return cum, state

    lax.fori_loop(
        0, tokens // 16, scan, (jnp.ones((1, own), f32), jnp.zeros((1, own), f32))
    )


def merge_kernel(state_ref, cum_ref, carry_ref, pre_ref, h_ref, merged_ref):
    def step(index, none):
        span = pl.ds(pl.multiple_of(index * 32, 32), 32)
        state = state_ref[0, span, :] + cum_ref[0, span, :] * carry_ref[0, 0:1]
        h_ref[0, span, :] = state
        merged_ref[0, span, :] = (state * gelu(pre_ref[0, span, :])).astype(bf16)
        return none

    lax.fori_loop(0, state_ref.shape[1] // 32, step, 0)


def adjoint_kernel(gm_ref, h_ref, pre_ref, decay_ref, gh_ref, gpre_ref, back_ref, cum_ref):
    tokens, own = gm_ref.shape[1:]
    row = rows_of((8, own))
    count = tokens // 16

    def step(index, carry):
        cum, back = carry
        start = pl.multiple_of((count - 1 - index) * 16, 16)
        span = pl.ds(start, 16)
        grad = gm_ref[0, span, :]
        act, slope = gelu_both(pre_ref[0, span, :])
        gpre_ref[0, span, :] = (grad * h_ref[0, span, :] * slope).astype(bf16)
        grad_h = grad * act
        gh_ref[0, span, :] = grad_h
        decay = decay_ref[0, span, :]
        driven = decay * grad_h
        for tile in (1, 0):
            a = decay[tile * 8 : tile * 8 + 8]
            b = driven[tile * 8 : tile * 8 + 8]
            for d in (1, 2, 4):
                there = row < 8 - d
                after_a = jnp.where(there, pltpu.roll(a, 8 - d, 0), 1.0)
                after_b = jnp.where(there, pltpu.roll(b, 8 - d, 0), 0.0)
                b = b + a * after_b
                a = a * after_a
            b = b + a * back
            a = a * cum
            place = pl.ds(start + tile * 8, 8)
            back_ref[0, place, :] = b
            cum_ref[0, place, :] = a
            cum, back = a[0:1], b[0:1]
        return cum, back

    lax.fori_loop(0, count, step, (jnp.ones((1, own), f32), jnp.zeros((1, own), f32)))


def backward_kernel(
    head, odd_ref, back_ref, cum_ref, gh_ref, h_ref, carry_ref, enter_ref, recur_ref, input_ref,
    decay_ref, conv_ref, u_ref, gy_ref, rim_ref, cw_ref, gw_ref, gs_ref, sp_ref,
    gu_ref, tail_ref, lead_ref, small_ref, taps_ref, gwg_ref, gsg_ref,
    padded, ahead, behind, low, gg, direct,
):
    tokens, wide = u_ref.shape[1:]
    own = recur_ref.shape[2]
    half = head // 2
    odd = odd_ref[0] == 1
    taps = cw_ref.shape[0]

    @pl.when(pl.program_id(0) == 0)
    def _():
        small_ref[...] = jnp.zeros_like(small_ref)
        taps_ref[...] = jnp.zeros_like(taps_ref)
        gwg_ref[...] = jnp.zeros_like(gwg_ref)
        gsg_ref[...] = jnp.zeros_like(gsg_ref)

    padded[0:8] = rim_ref[0]
    padded[8:] = u_ref[0]
    behind[0:8] = carry_ref[0]
    ahead[tokens:] = enter_ref[0]
    direct[tokens:] = jnp.zeros((8, wide), f32)
    enter = enter_ref[0, 0:1]

    def prepare(index, none):
        start = pl.multiple_of(index * 32, 32)
        span = pl.ds(start, 32)
        ahead[span, :] = back_ref[0, span, :] + cum_ref[0, span, :] * enter
        behind[pl.ds(start + 8, 32), :] = h_ref[0, span, :]
        return none

    lax.fori_loop(0, tokens // 32, prepare, 0)

    def gates(index, sums):
        sum_recur, sum_input, sum_decay = sums
        start = pl.multiple_of(index * 16, 16)
        span = pl.ds(start, 16)
        after = pltpu.roll(ahead[pl.ds(start, 24), :], 23, 0)[:16]
        before = pltpu.roll(behind[pl.ds(start, 24), :], 1, 0)[8:]
        adj = gh_ref[0, span, :] + after
        recur = recur_ref[0, span, :]
        gate = input_ref[0, span, :]
        decay = decay_ref[0, span, :]
        whole = conv_ref[0, span, :]
        low[span, :] = whole.astype(bf16)
        conv = jnp.concatenate([whole[:, : 2 * head], pick(odd, whole, half)], 1)
        square = one_less_square(2.0 * (recur * sp_ref[...]))
        inverse = lax.rsqrt(square)
        root = square * inverse
        grad_a = adj * before
        part = adj * gate
        grad_direct = part * root
        grad_gate = adj * conv * root
        grad_root = part * conv
        grad_log = decay * (grad_a - grad_root * decay * inverse)
        scaled = grad_log * recur
        grad_recur = scaled * sp_ref[...] * (1.0 - recur)
        grad_input = grad_gate * gate * (1.0 - gate)
        gg[0, span, :] = grad_recur.astype(bf16)
        gg[1, span, :] = grad_input.astype(bf16)
        shared = grad_direct[:, 2 * head :]
        none = jnp.zeros_like(shared)
        direct[span, :] = jnp.concatenate(
            [grad_direct[:, : 2 * head], jnp.where(odd, none, shared), jnp.where(odd, shared, none)],
            1,
        )
        fold = lambda old, new: old + new[:8] + new[8:]
        return fold(sum_recur, grad_recur), fold(sum_input, grad_input), fold(sum_decay, scaled)

    zero = jnp.zeros((8, own), f32)
    sums = lax.fori_loop(0, tokens // 16, gates, (zero, zero, zero))
    for position, value in enumerate(sums):
        small_ref[position : position + 1] += jnp.sum(value, axis=0, keepdims=True)
    across = (((1,), (1,)), ((), ()))
    down = (((0,), (0,)), ((), ()))
    for h in range(2):
        cols = slice(h * head, (h + 1) * head)
        direct[0:tokens, cols] += lax.dot_general(
            gg[0, :, cols], gw_ref[0, h], across, preferred_element_type=f32
        ) + lax.dot_general(gg[1, :, cols], gw_ref[1, h], across, preferred_element_type=f32)
        for g in range(2):
            gwg_ref[g, h] += lax.dot_general(
                low[:, cols], gg[g, :, cols], down, preferred_element_type=f32
            )
    direct[0:tokens, 2 * head :] += lax.dot_general(
        gg[0, :, 2 * head :], gs_ref[0], across, preferred_element_type=f32
    ) + lax.dot_general(gg[1, :, 2 * head :], gs_ref[1], across, preferred_element_type=f32)
    for g in range(2):
        gsg_ref[g] += lax.dot_general(
            low[:, 2 * head :], gg[g, :, 2 * head :], down, preferred_element_type=f32
        )

    def deconvolve(index, sums):
        start = pl.multiple_of(index * 16, 16)
        window = direct[pl.ds(start, 24), :]
        inputs = padded[pl.ds(start, 24), :]
        grad = window[:16]
        out = cw_ref[0:1] * grad
        fold = lambda old, new: old + new[:8] + new[8:]
        new = [fold(sums[0], grad), fold(sums[1], grad * inputs[8:])]
        for k in range(1, taps):
            out = out + cw_ref[k : k + 1] * pltpu.roll(window, 24 - k, 0)[:16]
            new.append(fold(sums[k + 1], grad * pltpu.roll(inputs, k, 0)[8:]))
        gu_ref[0, pl.ds(start, 16), :wide] = out.astype(bf16)
        gu_ref[0, pl.ds(start, 16), wide:] = gy_ref[0, pl.ds(start, 16), :]

        @pl.when(index == tokens // 16 - 1)
        def _():
            tail_ref[0] = out[8:]

        return tuple(new)

    zero = jnp.zeros((8, wide), f32)
    sums = lax.fori_loop(0, tokens // 16, deconvolve, (zero,) * (taps + 1))
    for position, value in enumerate(sums):
        taps_ref[position : position + 1] += jnp.sum(value, axis=0, keepdims=True)
    first = direct[0:8, :]
    row = rows_of((8, wide))
    owed = jnp.zeros((8, wide), f32)
    for k in range(1, taps):
        moved = pltpu.roll(first, 8 - k, 0)
        owed = owed + cw_ref[k : k + 1] * jnp.where(row >= 8 - k, moved, 0.0)
    lead_ref[0] = owed


def mlp_kernel(normed_ref, weight_ref, grad_ref, hidden_ref, out_ref):
    part = hidden_ref.shape[1]
    rows = 512

    def step(index, none):
        span = pl.ds(pl.multiple_of(index * rows, rows), rows)
        both = jnp.dot(normed_ref[span, :], weight_ref[...], preferred_element_type=f32)
        act, slope = gelu_both(both[:, :part])
        up = both[:, part:]
        grad = grad_ref[span, :].astype(f32)
        hidden_ref[span, :] = (act * up).astype(bf16)
        out_ref[span, :part] = (grad * up * slope).astype(bf16)
        out_ref[span, part:] = (grad * act).astype(bf16)
        return none

    lax.fori_loop(0, normed_ref.shape[0] // rows, step, 0)


def spread_mlp_kernel(layout, mine_ref, a_ref, b_ref, c_ref, d_ref, out_ref):
    parts, per_part, fine = layout
    blocks = (a_ref, b_ref, c_ref, d_ref)
    part = per_part * fine
    span = part * len(blocks)
    for mine in range(len(blocks)):

        @pl.when(mine_ref[0] == mine)
        def _(mine=mine):
            for p in range(parts):
                for h in range(2):
                    base = (2 * p + h) * part
                    wholes = [blocks[k][:, base : base + part].astype(f32) for k in range(len(blocks))]
                    pieces = [
                        wholes[mine ^ a][:, g * fine : (g + 1) * fine]
                        for g in range(per_part)
                        for a in range(len(blocks))
                    ]
                    at = (h * parts + p) * span
                    out_ref[:, at : at + span] = jnp.concatenate(pieces, 1)


def spread_in_kernel(head, mine_ref, a_ref, b_ref, c_ref, d_ref, out_ref):
    blocks = (a_ref, b_ref, c_ref, d_ref)
    half = head // 2
    wide = 3 * head
    rec = out_ref.shape[1] // 2
    for mine in range(len(blocks)):

        @pl.when(mine_ref[0] == mine)
        def _(mine=mine):
            for k, block in enumerate(blocks):
                member = mine ^ k
                first, shared = 5 * (member // 2) + 3 * (member % 2), 5 * (member // 2) + 2
                at = first * head
                out_ref[:, at : at + 2 * head] = block[:, : 2 * head].astype(f32)
                out_ref[:, rec + at : rec + at + 2 * head] = block[:, wide : wide + 2 * head].astype(f32)
                at = rec + shared * head + (member % 2) * half
                out_ref[:, at : at + half] = block[:, wide + 2 * head :].astype(f32)
                if k % 2 == 0:
                    at = shared * head
                    out_ref[:, at : at + head] = block[:, 2 * head : wide].astype(f32) + blocks[k + 1][
                        :, 2 * head : wide
                    ].astype(f32)


def spread(kernel, mine, blocks, columns, name):
    rows, wide = blocks[0].shape
    step = min(32, rows)
    piece = pl.BlockSpec((step, wide), lambda i: (i, 0))
    return pl.pallas_call(
        kernel,
        grid=(rows // step,),
        in_specs=[SCALAR] + [piece] * len(blocks),
        out_specs=pl.BlockSpec((step, columns), lambda i: (i, 0)),
        out_shape=jax.ShapeDtypeStruct((rows, columns), f32),
        compiler_params=params("arbitrary"),
        cost_estimate=cost(8),
        name=name,
    )(mine.astype(jnp.int32).reshape(1), *blocks)


def params(*semantics):
    return pltpu.CompilerParams(dimension_semantics=semantics, vmem_limit_bytes=VMEM_LIMIT)


def per_seq(*shape):
    return pl.BlockSpec((1, *shape), lambda i: (i,) + (0,) * len(shape))


def whole(*shape):
    return pl.BlockSpec(shape, lambda i: (0,) * len(shape))


SCALAR = pl.BlockSpec(memory_space=pltpu.SMEM)


def cost(microseconds):
    return pl.CostEstimate(
        flops=int(microseconds * 1e9), bytes_accessed=int(microseconds * 3e6), transcendentals=0
    )


def shards(
    block_input,
    out_cotangent,
    norm_gain,
    in_weight,
    conv_weight,
    conv_bias,
    gate_weight,
    gate_bias,
    decay_param,
    out_weight,
    mlp_gain,
    mlp_weight,
    down_weight,
):
    _, tokens, model = block_input.shape
    taps, rec = conv_weight.shape
    heads, head = gate_weight.shape[1:3]
    members = lax.axis_size("seq")
    devices = lax.axis_size("group")
    hidden = mlp_weight.shape[1] // 2
    assert members == 4 and heads == 10
    half = head // 2
    own = 2 * head + half
    wide = 3 * head
    mine = lax.axis_index("seq")
    odd = mine % 2

    def first_of(member):
        return 5 * (member // 2) + 3 * (member % 2), 5 * (member // 2) + 2

    first, shared = first_of(mine)

    def widen(value, offset=0):
        return jnp.concatenate(
            [
                lax.dynamic_slice_in_dim(value, offset + first * head, 2 * head, value.ndim - 1),
                lax.dynamic_slice_in_dim(value, offset + shared * head, head, value.ndim - 1),
            ],
            -1,
        )

    def owned(value, offset=0):
        return jnp.concatenate(
            [
                lax.dynamic_slice_in_dim(value, offset + first * head, 2 * head, value.ndim - 1),
                lax.dynamic_slice_in_dim(
                    value, offset + shared * head + odd * half, half, value.ndim - 1
                ),
            ],
            -1,
        )

    in_cols = gather_group(jnp.concatenate([widen(in_weight), owned(in_weight, rec)], 1))
    in_u, in_y = in_cols[:, :wide], in_cols[:, wide:]
    x_own = block_input[0]
    x_blocks = gather_seq(x_own)
    x_all = jnp.concatenate(x_blocks, 0)
    c_own = after(out_cotangent[0], x_blocks[1])
    c_blocks = gather_seq(c_own)
    c_all = jnp.concatenate(c_blocks, 0)
    fine = hidden // devices // members
    part = min(384, hidden // members)
    per_part = part // fine
    parts = hidden // members // part
    cut = after(mlp_weight, x_blocks[1]).reshape(-1, 2, parts, per_part, members, fine)
    cut = lax.dynamic_index_in_dim(cut, mine, 4, keepdims=False)
    cut = cut.transpose(0, 2, 1, 3, 4).reshape(mlp_weight.shape[0], -1)
    normed = after(rms_low(x_all.astype(f32), norm_gain), cut)
    out_piece = model // members
    out_cols = gather_group(
        after(lax.dynamic_slice_in_dim(out_weight, mine * out_piece, out_piece, 1), in_cols, normed)
    )
    def rows_for(value, k):
        start, common = first_of(mine ^ k)
        return jnp.concatenate(
            [
                lax.dynamic_slice_in_dim(value, start * head, 2 * head, 0),
                lax.dynamic_slice_in_dim(
                    value, common * head + ((mine ^ k) % 2) * half, half, 0
                ),
            ],
            0,
        )

    out_rows = jnp.zeros((own, model), bf16)
    for k in range(members):
        piece = rows_for(out_cols, k)
        if k:
            piece = swap(piece, k)
        out_rows = lax.dynamic_update_slice_in_dim(out_rows, piece, (mine ^ k) * out_piece, 1)

    u = jnp.dot(normed, in_u, preferred_element_type=f32).reshape(members, tokens, wide)
    u = after(u, c_blocks[1], c_blocks[2])
    y = jnp.dot(normed, in_y, preferred_element_type=f32).reshape(members, tokens, own)
    lead = taps - 1
    rim = jnp.pad(shift(u[:, tokens - lead :], 1), ((0, 0), (8 - lead, 0), (0, 0)))
    odd_flag = odd.astype(jnp.int32).reshape(1)
    cw = widen(conv_weight)
    cb = widen(conv_bias)[None]
    gb = owned(gate_bias)
    soft = -8.0 * owned(jax.nn.softplus(decay_param))[None]
    gw = lax.dynamic_slice_in_dim(gate_weight, first, 2, 1)
    gs = lax.dynamic_slice(
        gate_weight, (0, shared, 0, odd * half), (2, 1, head, half)
    )[:, 0]
    rows = members * tokens
    full = jax.ShapeDtypeStruct((members, tokens, own), f32)
    conv, recur, gate, decay, state_local, decay_cum = pl.pallas_call(
        functools.partial(forward_kernel, head),
        grid=(members,),
        in_specs=[
            SCALAR,
            per_seq(tokens, wide),
            per_seq(8, wide),
            whole(taps, wide),
            whole(1, wide),
            whole(2, 2, head, head),
            whole(2, head, half),
            whole(2, own),
            whole(1, own),
        ],
        out_specs=[per_seq(tokens, wide)] + [per_seq(tokens, own)] * 5,
        out_shape=[jax.ShapeDtypeStruct((members, tokens, wide), f32)] + [full] * 5,
        scratch_shapes=[
            pltpu.VMEM((tokens + 8, wide), f32),
            pltpu.VMEM((tokens, wide), bf16),
            pltpu.VMEM((2, tokens, own), f32),
        ],
        compiler_params=params("arbitrary"),
        cost_estimate=cost(14),
        name="recurrence_forward",
    )(odd_flag, u, rim, cw, cb, gw, gs, gb, soft)
    down_rows = gather_group(
        after(
            lax.dynamic_slice_in_dim(down_weight, mine * fine, fine, 0), out_cols, u
        )
    )
    carried = entering(decay_cum[:, -1], state_local[:, -1], 1)
    arrived = carried
    carried = after(carried, out_rows)
    carried8 = jnp.broadcast_to(carried[:, None], (members, 8, own))
    h, merged = pl.pallas_call(
        merge_kernel,
        grid=(members,),
        in_specs=[per_seq(tokens, own)] * 2 + [per_seq(8, own), per_seq(tokens, own)],
        out_specs=[per_seq(tokens, own)] * 2,
        out_shape=[full, jax.ShapeDtypeStruct((members, tokens, own), bf16)],
        compiler_params=params("arbitrary"),
        cost_estimate=cost(14),
        name="recurrence_merge",
    )(state_local, decay_cum, carried8, y)
    partial = jnp.dot(merged.reshape(rows, own), out_rows, preferred_element_type=f32)
    partial = partial.astype(bf16)
    mlp_cols = gather_group(after(cut, down_rows, out_rows, arrived))
    partial = lax.optimization_barrier(partial).reshape(members, tokens, model)
    x32 = x_own.astype(f32)
    grad_hidden = lax.dot_general(
        c_all, down_rows, (((1,), (1,)), ((), ())), preferred_element_type=f32
    )
    resid = after(x32 + scatter_seq(partial), grad_hidden)
    normed2 = jnp.concatenate(gather_seq(rms_low(resid, mlp_gain)), 0)

    width = parts * part
    hidden_low, grad_gu = pl.pallas_call(
        mlp_kernel,
        grid=(parts,),
        in_specs=[
            whole(rows, model),
            pl.BlockSpec((model, 2 * part), lambda i: (0, i)),
            pl.BlockSpec((rows, part), lambda i: (0, i)),
        ],
        out_specs=[
            pl.BlockSpec((rows, part), lambda i: (0, i)),
            pl.BlockSpec((rows, 2 * part), lambda i: (0, i)),
        ],
        out_shape=[
            jax.ShapeDtypeStruct((rows, width), bf16),
            jax.ShapeDtypeStruct((rows, 2 * width), bf16),
        ],
        compiler_params=params("arbitrary"),
        cost_estimate=pl.CostEstimate(
            flops=4 * rows * model * width,
            bytes_accessed=rows * model * 2 + model * width * 4 + rows * width * 10,
            transcendentals=rows * width,
        ),
        name="mlp",
    )(normed2, mlp_cols, grad_hidden)
    across = (((1,), (1,)), ((), ()))
    down = (((0,), (0,)), ((), ()))
    down_part = lax.dot_general(hidden_low, c_all, down, preferred_element_type=f32).astype(bf16)
    down_sum = scatter_group(down_part)
    partial = lax.dot_general(
        after(grad_gu, down_part), mlp_cols, across, preferred_element_type=f32
    ).astype(bf16)
    mlp_part = lax.dot_general(
        normed2, after(grad_gu, partial), down, preferred_element_type=f32
    ).astype(bf16)
    grad_normed2 = scatter_seq(lax.optimization_barrier(partial).reshape(members, tokens, model))
    final = jnp.dot(
        after(hidden_low, mlp_part), down_rows, preferred_element_type=f32
    ).astype(bf16)
    grad_normed2 = after(grad_normed2, final)
    grad_resid_norm, mlp_gain_grad = rms_back(resid, mlp_gain, grad_normed2)
    grad_resid = c_own.astype(f32) + grad_resid_norm
    grad_resid_all = jnp.concatenate(gather_seq(grad_resid.astype(bf16)), 0)
    mlp_sum = scatter_group(after(mlp_part, down_sum, grad_normed2))

    final = after(final, grad_resid_all).reshape(members, tokens, model)
    final_hop = first_hop(final[3])
    block_out = (resid + scatter_seq(final, final_hop)).astype(bf16)[None]
    grad_merged = lax.dot_general(
        grad_resid_all, out_rows, (((1,), (1,)), ((), ())), preferred_element_type=f32
    ).reshape(members, tokens, own)
    grad_merged = after(grad_merged, *final_hop)
    down_first = after(down_sum, *final_hop)
    down_hop = swap(down_first, 1), swap(down_first, 2)
    grad_h, grad_y, back_local, back_cum = pl.pallas_call(
        adjoint_kernel,
        grid=(members,),
        in_specs=[per_seq(tokens, own)] * 4,
        out_specs=[per_seq(tokens, own)] * 4,
        out_shape=[full, jax.ShapeDtypeStruct((members, tokens, own), bf16), full, full],
        compiler_params=params("arbitrary"),
        cost_estimate=cost(10),
        name="recurrence_adjoint",
    )(grad_merged, h, y, decay)
    incoming = entering(back_cum[:, 0], back_local[:, 0], -1)
    incoming8 = jnp.broadcast_to(incoming[:, None], (members, 8, own))
    grad_proj, tail, owed, small, tap_sums, gw_grad, gs_grad = pl.pallas_call(
        functools.partial(backward_kernel, head),
        grid=(members,),
        in_specs=[
            SCALAR,
            *[per_seq(tokens, own)] * 4,
            per_seq(8, own),
            per_seq(8, own),
            *[per_seq(tokens, own)] * 3,
            *[per_seq(tokens, wide)] * 2,
            per_seq(tokens, own),
            per_seq(8, wide),
            whole(taps, wide),
            whole(2, 2, head, head),
            whole(2, head, half),
            whole(1, own),
        ],
        out_specs=[
            per_seq(tokens, wide + own),
            per_seq(8, wide),
            per_seq(8, wide),
            whole(8, own),
            whole(8, wide),
            whole(2, 2, head, head),
            whole(2, head, half),
        ],
        out_shape=[
            jax.ShapeDtypeStruct((members, tokens, wide + own), bf16),
            jax.ShapeDtypeStruct((members, 8, wide), f32),
            jax.ShapeDtypeStruct((members, 8, wide), f32),
            jax.ShapeDtypeStruct((8, own), f32),
            jax.ShapeDtypeStruct((8, wide), f32),
            jax.ShapeDtypeStruct((2, 2, head, head), f32),
            jax.ShapeDtypeStruct((2, head, half), f32),
        ],
        scratch_shapes=[
            pltpu.VMEM((tokens + 8, wide), f32),
            pltpu.VMEM((tokens + 8, own), f32),
            pltpu.VMEM((tokens + 8, own), f32),
            pltpu.VMEM((tokens, wide), bf16),
            pltpu.VMEM((2, tokens, own), bf16),
            pltpu.VMEM((tokens + 8, wide), f32),
        ],
        compiler_params=params("arbitrary"),
        cost_estimate=cost(19),
        name="recurrence_backward",
    )(
        odd_flag, back_local, back_cum, grad_h, h, carried8, incoming8, recur, gate,
        decay, conv, u, grad_y, rim, cw, gw, gs, soft,
    )
    tail = (tail + shift(owed, -1)).astype(bf16)
    grad_proj = lax.dynamic_update_slice(grad_proj, tail, (0, tokens - 8, 0))
    grad_proj = grad_proj.reshape(rows, wide + own)
    out_part = lax.dot_general(
        merged.reshape(rows, own), grad_resid_all, down, preferred_element_type=f32
    ).astype(bf16)
    pieces = []
    for k in range(members):
        piece = lax.dynamic_slice_in_dim(out_part, (mine ^ k) * out_piece, out_piece, 1)
        pieces.append(swap(piece, k) if k else piece)
    pieces = jnp.stack(pieces)
    out_terms = []
    for member in range(members):
        piece = lax.dynamic_index_in_dim(pieces, mine ^ member, 0, keepdims=False)
        cut_at = 2 * head if member % 2 else 0
        out_terms += [piece[cut_at:], piece[:cut_at]]
    out_terms = jnp.concatenate(out_terms, 0)
    gate_terms = jnp.concatenate([gw_grad[:, 0], gw_grad[:, 1], gs_grad], -1).reshape(-1, own)
    decay_terms = small[2:3] * (-8.0) * owned(jax.nn.sigmoid(decay_param))[None]
    sizes = ((taps + 1) * wide, 3 * own, model)
    small_terms = jnp.concatenate(
        [
            tap_sums[: taps + 1].reshape(-1),
            small[:2].reshape(-1),
            decay_terms.reshape(-1),
            mlp_gain_grad,
        ]
    )
    small_rows = 64
    small_terms = jnp.pad(small_terms, (0, small_rows * own - small_terms.shape[0]))
    terms = jnp.concatenate([gate_terms, small_terms.reshape(small_rows, own)], 0).astype(bf16)
    group_terms = total_group(terms)
    partial = lax.dot_general(
        after(grad_proj, out_terms, *down_hop, group_terms), in_cols, across, preferred_element_type=f32
    )
    partial = lax.optimization_barrier(partial.astype(bf16)).reshape(members, tokens, model)
    hop = first_hop(partial[3])
    out_sum = scatter_group(after(out_terms, mlp_sum, grad_proj))
    in_part = lax.dot_general(normed, grad_proj, down, preferred_element_type=f32).astype(bf16)
    in_sum = scatter_group(after(in_part, out_sum, *hop))

    out_blocks = gather_seq(out_sum)
    grad_normed = scatter_seq(partial, (after(hop[0], out_sum), after(hop[1], out_sum)))
    mlp_late = after(mlp_sum, out_sum)
    mlp_hop = swap(mlp_late, 1), swap(mlp_late, 2)
    term_parts = gather_seq(after(group_terms, *hop))
    gate_parts = [after(piece[: 2 * head], in_sum) for piece in term_parts]
    small_parts = jnp.stack([piece[2 * head :].reshape(-1) for piece in term_parts])
    grad_input_norm, norm_gain_grad = rms_back(x32, norm_gain, grad_normed)
    input_grad = (grad_resid + grad_input_norm)[None]

    mlp_blocks = gather_seq(mlp_late, mlp_hop)
    mlp_grad = spread(
        functools.partial(spread_mlp_kernel, (parts, per_part, fine)),
        mine,
        mlp_blocks,
        2 * hidden,
        "spread_mlp",
    )
    out_parts = jnp.stack(out_blocks)
    out_grad = jnp.concatenate(
        [lax.dynamic_index_in_dim(out_parts, mine ^ a, 0, keepdims=False) for a in range(members)],
        1,
    ).astype(f32)
    down_parts = jnp.stack(gather_seq(down_sum, down_hop))
    down_grad = jnp.concatenate(
        [lax.dynamic_index_in_dim(down_parts, mine ^ a, 0, keepdims=False) for a in range(members)],
        0,
    ).astype(f32)
    gate_grad = jnp.zeros((2, heads, head, head), f32)
    for k in range(members):
        start, common = first_of(mine ^ k)
        block = gate_parts[k].reshape(2, head, own).astype(f32)
        pair = block[:, :, : 2 * head].reshape(2, head, 2, head).transpose(0, 2, 1, 3)
        gate_grad = lax.dynamic_update_slice_in_dim(gate_grad, pair, start, 1)
        if k % 2 == 0:
            other = gate_parts[k + 1].reshape(2, head, own).astype(f32)
            halves = jnp.where(
                odd == 1,
                jnp.concatenate([other[..., 2 * head :], block[..., 2 * head :]], -1),
                jnp.concatenate([block[..., 2 * head :], other[..., 2 * head :]], -1),
            )
            gate_grad = lax.dynamic_update_slice_in_dim(gate_grad, halves[:, None], common, 1)

    def place(value, member, wide_shared):
        start, common = first_of(member)
        at = common * head if wide_shared else common * head + (member % 2) * half
        out = jnp.zeros((value.shape[0], rec), f32)
        out = lax.dynamic_update_slice_in_dim(out, value[:, : 2 * head], start * head, 1)
        return lax.dynamic_update_slice_in_dim(out, value[:, 2 * head :], at, 1)

    tap_grads, own_grads, mlp_gain_grad = 0.0, 0.0, 0.0
    for member in range(members):
        piece = lax.dynamic_index_in_dim(small_parts, mine ^ member, 0, keepdims=False).astype(f32)
        one, two, three, _ = jnp.split(
            piece, (sizes[0], sizes[0] + sizes[1], sizes[0] + sizes[1] + sizes[2])
        )
        tap_grads = tap_grads + place(one.reshape(-1, wide), member, True)
        own_grads = own_grads + place(two.reshape(-1, own), member, False)
        mlp_gain_grad = mlp_gain_grad + three
    norm_gain_grad = total(norm_gain_grad.reshape(-1, 128)).reshape(-1)
    in_grad = spread(
        functools.partial(spread_in_kernel, head), mine, gather_seq(after(in_sum, *mlp_hop, *out_blocks, *term_parts)), 2 * rec, "spread_in"
    )

    return (
        block_out,
        input_grad,
        norm_gain_grad,
        in_grad,
        tap_grads[1:],
        tap_grads[0],
        gate_grad,
        own_grads[:2],
        own_grads[2],
        out_grad,
        mlp_gain_grad,
        mlp_grad,
        down_grad,
    )


def solution(mesh):
    tokens = P("seq", "group", None)
    rows = P("group", None)
    in_specs = (tokens, tokens, P(), rows, P(), P(), P(), P(), P(), rows, P(), rows, rows)
    out_specs = (tokens, tokens, P(), rows, P(), P(), P(), P(), P(), rows, P(), rows, rows)
    return jax.shard_map(shards, mesh=mesh, in_specs=in_specs, out_specs=out_specs, check_vma=False)
```

```python
import functools

import jax
import jax.numpy as jnp
from jax import lax
from jax.experimental import pallas as pl
from jax.experimental.pallas import tpu as pltpu
from jax.sharding import PartitionSpec as P

epsilon = 1e-06
f32 = jnp.float32
bf16 = jnp.bfloat16
VMEM_LIMIT = 58 * 1024 * 1024


def swap(block, k):
    return lax.ppermute(block, "seq", [(i, i ^ k) for i in range(lax.axis_size("seq"))])


def shift(block, distance):
    devices = range(lax.axis_size("group"))
    return lax.ppermute(
        block, "group", [(i - distance, i) for i in devices if i - distance in devices]
    )


def gather_seq(block, hop=None):
    half = block.shape[0] // 2
    first, second = (swap(block, 1), swap(block, 2)) if hop is None else hop
    third = jnp.concatenate([swap(first[:half], 2), swap(second[half:], 1)], 0)
    return [block, first, second, third]


def first_hop(third):
    half = third.shape[0] // 2
    return swap(third[:half], 1), swap(third[half:], 2)


def scatter_seq(parts, hop=None):
    half = parts[0].shape[0] // 2
    own, first, second, third = parts
    top, bottom = first_hop(third) if hop is None else hop
    first_top = swap(first[:half], 1)
    second_bottom = swap(second[half:], 2)
    second_top = swap((second[:half].astype(f32) + top.astype(f32)).astype(bf16), 2)
    first_bottom = swap((first[half:].astype(f32) + bottom.astype(f32)).astype(bf16), 1)
    return jnp.concatenate(
        [
            own[:half].astype(f32) + first_top.astype(f32) + second_top.astype(f32),
            own[half:].astype(f32) + first_bottom.astype(f32) + second_bottom.astype(f32),
        ],
        0,
    )


def gather_group(block):
    return lax.all_gather(block, "group", axis=0, tiled=True)


def scatter_group(block):
    return lax.psum_scatter(block, "group", scatter_dimension=0, tiled=True)


def after(value, *others):
    return lax.optimization_barrier((value, *others))[0]


def total_group(value):
    count = lax.axis_size("group")
    place = lax.axis_index("group")
    route = lambda step: [(i, i ^ step) for i in range(count)]
    steps = [1 << i for i in range(count.bit_length() - 1)]
    for step in steps:
        half = value.shape[0] // 2
        bit = (place // step) % 2
        kept = lax.dynamic_slice_in_dim(value, bit * half, half, 0)
        given = lax.dynamic_slice_in_dim(value, (1 - bit) * half, half, 0)
        got = lax.ppermute(given, "group", route(step))
        value = (kept.astype(f32) + got.astype(f32)).astype(value.dtype)
    for step in reversed(steps):
        bit = (place // step) % 2
        got = lax.ppermute(value, "group", route(step))
        value = jnp.where(
            bit == 0, jnp.concatenate([value, got], 0), jnp.concatenate([got, value], 0)
        )
    return value


def total(value):
    for axis in ("group", "seq"):
        count = lax.axis_size(axis)
        step = 1
        while step < count:
            value = value + lax.ppermute(value, axis, [(i, i ^ step) for i in range(count)])
            step *= 2
    return value


def link(earlier, later):
    return (earlier[0] * later[0], later[1] + later[0] * earlier[1])


def entering(decay, state, sign):
    count = lax.axis_size("group")
    pair = jnp.stack([decay, state])
    near = [shift(pair, sign * distance) for distance in range(1, min(4, count - 1) + 1)]
    decay, state = near[0][0], near[0][1]
    for before in near[1:]:
        decay, state = link((before[0], before[1]), (decay, state))
    covered = len(near)
    while covered < count - 1:
        before = shift(jnp.stack([decay, state]), sign * covered)
        decay, state = link((before[0], before[1]), (decay, state))
        covered *= 2
    return state


def rms_low(value, gain):
    scale = lax.rsqrt(jnp.mean(value * value, axis=-1, keepdims=True) + epsilon)
    return (value * scale * gain).astype(bf16)


def rms_back(value, gain, grad):
    width = value.shape[-1]
    scale = lax.rsqrt(jnp.mean(value * value, axis=-1, keepdims=True) + epsilon)
    scaled = grad * gain
    along = jnp.sum(scaled * value, axis=-1, keepdims=True) / width
    grad_value = scale * scaled - value * (scale * scale * scale * along)
    grad_gain = jnp.sum(grad * value * scale, axis=0)
    return grad_value, grad_gain


ROOT = 0.7978845608028654
CUBE = 0.044715


def gelu(v):
    return 0.5 * v * (1.0 + jnp.tanh(ROOT * (v + CUBE * v * v * v)))


def gelu_both(v):
    square = v * v
    t = jnp.tanh(ROOT * v * (1.0 + CUBE * square))
    half = 0.5 * (1.0 + t)
    slope = half + 0.5 * v * (1.0 - t * t) * (ROOT * (1.0 + 3.0 * CUBE * square))
    return v * half, slope


def one_less_square(double):
    series = jnp.full_like(double, 1.0 / 362880.0)
    for term in (40320.0, 5040.0, 720.0, 120.0, 24.0, 6.0, 2.0, 1.0):
        series = series * double + 1.0 / term
    return -double * series


def rows_of(shape):
    return lax.broadcasted_iota(jnp.int32, shape, 0)


def pick(odd, value, width):
    lanes = value.shape[-1]
    return jnp.where(odd, value[:, lanes - width :], value[:, lanes - 2 * width : lanes - width])


def forward_kernel(
    head, odd_ref, u_ref, rim_ref, cw_ref, cb_ref, gw_ref, gs_ref, gb_ref, sp_ref,
    conv_ref, recur_ref, input_ref, decay_ref, state_ref, cum_ref,
    padded, low, pre,
):
    tokens, wide = u_ref.shape[1:]
    own = recur_ref.shape[2]
    odd = odd_ref[0] == 1
    padded[0:8] = rim_ref[0]
    padded[8:] = u_ref[0]
    taps = cw_ref.shape[0]

    def convolve(index, carry):
        start = pl.multiple_of(index * 32, 32)
        window = padded[pl.ds(start, 40), :]
        out = cb_ref[...] + cw_ref[0:1] * window[8:]
        for k in range(1, taps):
            out = out + cw_ref[k : k + 1] * pltpu.roll(window, k, 0)[8:]
        conv_ref[0, pl.ds(start, 32), :] = out
        low[pl.ds(start, 32), :] = out.astype(bf16)
        return carry

    lax.fori_loop(0, tokens // 32, convolve, 0)
    for g in range(2):
        for h in range(2):
            cols = slice(h * head, (h + 1) * head)
            pre[g, :, cols] = jnp.dot(low[:, cols], gw_ref[g, h], preferred_element_type=f32)
        pre[g, :, 2 * head :] = jnp.dot(low[:, 2 * head :], gs_ref[g], preferred_element_type=f32)
    row = rows_of((8, own))

    def scan(index, carry):
        cum, state = carry
        start = pl.multiple_of(index * 16, 16)
        span = pl.ds(start, 16)
        recur = jax.nn.sigmoid(pre[0, span, :] + gb_ref[0:1])
        gate = jax.nn.sigmoid(pre[1, span, :] + gb_ref[1:2])
        log_decay = recur * sp_ref[...]
        decay = jnp.exp(log_decay)
        conv = conv_ref[0, span, :]
        conv = jnp.concatenate([conv[:, : 2 * head], pick(odd, conv, head // 2)], 1)
        driven = conv * gate * jnp.sqrt(one_less_square(2.0 * log_decay))
        recur_ref[0, span, :] = recur
        input_ref[0, span, :] = gate
        decay_ref[0, span, :] = decay
        for tile in range(2):
            a = decay[tile * 8 : tile * 8 + 8]
            b = driven[tile * 8 : tile * 8 + 8]
            for d in (1, 2, 4):
                there = row >= d
                before_a = jnp.where(there, pltpu.roll(a, d, 0), 1.0)
                before_b = jnp.where(there, pltpu.roll(b, d, 0), 0.0)
                b = b + a * before_b
                a = a * before_a
            b = b + a * state
            a = a * cum
            place = pl.ds(start + tile * 8, 8)
            state_ref[0, place, :] = b
            cum_ref[0, place, :] = a
            cum, state = a[7:8], b[7:8]
        return cum, state

    lax.fori_loop(
        0, tokens // 16, scan, (jnp.ones((1, own), f32), jnp.zeros((1, own), f32))
    )


def merge_kernel(state_ref, cum_ref, carry_ref, pre_ref, h_ref, merged_ref):
    def step(index, none):
        span = pl.ds(pl.multiple_of(index * 32, 32), 32)
        state = state_ref[0, span, :] + cum_ref[0, span, :] * carry_ref[0, 0:1]
        h_ref[0, span, :] = state
        merged_ref[0, span, :] = (state * gelu(pre_ref[0, span, :])).astype(bf16)
        return none

    lax.fori_loop(0, state_ref.shape[1] // 32, step, 0)


def adjoint_kernel(gm_ref, h_ref, pre_ref, decay_ref, gh_ref, gpre_ref, back_ref, cum_ref):
    tokens, own = gm_ref.shape[1:]
    row = rows_of((8, own))
    count = tokens // 16

    def step(index, carry):
        cum, back = carry
        start = pl.multiple_of((count - 1 - index) * 16, 16)
        span = pl.ds(start, 16)
        grad = gm_ref[0, span, :]
        act, slope = gelu_both(pre_ref[0, span, :])
        gpre_ref[0, span, :] = (grad * h_ref[0, span, :] * slope).astype(bf16)
        grad_h = grad * act
        gh_ref[0, span, :] = grad_h
        decay = decay_ref[0, span, :]
        driven = decay * grad_h
        for tile in (1, 0):
            a = decay[tile * 8 : tile * 8 + 8]
            b = driven[tile * 8 : tile * 8 + 8]
            for d in (1, 2, 4):
                there = row < 8 - d
                after_a = jnp.where(there, pltpu.roll(a, 8 - d, 0), 1.0)
                after_b = jnp.where(there, pltpu.roll(b, 8 - d, 0), 0.0)
                b = b + a * after_b
                a = a * after_a
            b = b + a * back
            a = a * cum
            place = pl.ds(start + tile * 8, 8)
            back_ref[0, place, :] = b
            cum_ref[0, place, :] = a
            cum, back = a[0:1], b[0:1]
        return cum, back

    lax.fori_loop(0, count, step, (jnp.ones((1, own), f32), jnp.zeros((1, own), f32)))


def backward_kernel(
    head, odd_ref, back_ref, cum_ref, gh_ref, h_ref, carry_ref, enter_ref, recur_ref, input_ref,
    decay_ref, conv_ref, u_ref, gy_ref, rim_ref, cw_ref, gw_ref, gs_ref, sp_ref,
    gu_ref, tail_ref, lead_ref, small_ref, taps_ref, gwg_ref, gsg_ref,
    padded, ahead, behind, low, gg, direct,
):
    tokens, wide = u_ref.shape[1:]
    own = recur_ref.shape[2]
    half = head // 2
    odd = odd_ref[0] == 1
    taps = cw_ref.shape[0]

    @pl.when(pl.program_id(0) == 0)
    def _():
        small_ref[...] = jnp.zeros_like(small_ref)
        taps_ref[...] = jnp.zeros_like(taps_ref)
        gwg_ref[...] = jnp.zeros_like(gwg_ref)
        gsg_ref[...] = jnp.zeros_like(gsg_ref)

    padded[0:8] = rim_ref[0]
    padded[8:] = u_ref[0]
    behind[0:8] = carry_ref[0]
    ahead[tokens:] = enter_ref[0]
    direct[tokens:] = jnp.zeros((8, wide), f32)
    enter = enter_ref[0, 0:1]

    def prepare(index, none):
        start = pl.multiple_of(index * 32, 32)
        span = pl.ds(start, 32)
        ahead[span, :] = back_ref[0, span, :] + cum_ref[0, span, :] * enter
        behind[pl.ds(start + 8, 32), :] = h_ref[0, span, :]
        return none

    lax.fori_loop(0, tokens // 32, prepare, 0)

    def gates(index, sums):
        sum_recur, sum_input, sum_decay = sums
        start = pl.multiple_of(index * 16, 16)
        span = pl.ds(start, 16)
        after = pltpu.roll(ahead[pl.ds(start, 24), :], 23, 0)[:16]
        before = pltpu.roll(behind[pl.ds(start, 24), :], 1, 0)[8:]
        adj = gh_ref[0, span, :] + after
        recur = recur_ref[0, span, :]
        gate = input_ref[0, span, :]
        decay = decay_ref[0, span, :]
        whole = conv_ref[0, span, :]
        low[span, :] = whole.astype(bf16)
        conv = jnp.concatenate([whole[:, : 2 * head], pick(odd, whole, half)], 1)
        square = one_less_square(2.0 * (recur * sp_ref[...]))
        inverse = lax.rsqrt(square)
        root = square * inverse
        grad_a = adj * before
        part = adj * gate
        grad_direct = part * root
        grad_gate = adj * conv * root
        grad_root = part * conv
        grad_log = decay * (grad_a - grad_root * decay * inverse)
        scaled = grad_log * recur
        grad_recur = scaled * sp_ref[...] * (1.0 - recur)
        grad_input = grad_gate * gate * (1.0 - gate)
        gg[0, span, :] = grad_recur.astype(bf16)
        gg[1, span, :] = grad_input.astype(bf16)
        shared = grad_direct[:, 2 * head :]
        none = jnp.zeros_like(shared)
        direct[span, :] = jnp.concatenate(
            [grad_direct[:, : 2 * head], jnp.where(odd, none, shared), jnp.where(odd, shared, none)],
            1,
        )
        fold = lambda old, new: old + new[:8] + new[8:]
        return fold(sum_recur, grad_recur), fold(sum_input, grad_input), fold(sum_decay, scaled)

    zero = jnp.zeros((8, own), f32)
    sums = lax.fori_loop(0, tokens // 16, gates, (zero, zero, zero))
    for position, value in enumerate(sums):
        small_ref[position : position + 1] += jnp.sum(value, axis=0, keepdims=True)
    across = (((1,), (1,)), ((), ()))
    down = (((0,), (0,)), ((), ()))
    for h in range(2):
        cols = slice(h * head, (h + 1) * head)
        direct[0:tokens, cols] += lax.dot_general(
            gg[0, :, cols], gw_ref[0, h], across, preferred_element_type=f32
        ) + lax.dot_general(gg[1, :, cols], gw_ref[1, h], across, preferred_element_type=f32)
        for g in range(2):
            gwg_ref[g, h] += lax.dot_general(
                low[:, cols], gg[g, :, cols], down, preferred_element_type=f32
            )
    direct[0:tokens, 2 * head :] += lax.dot_general(
        gg[0, :, 2 * head :], gs_ref[0], across, preferred_element_type=f32
    ) + lax.dot_general(gg[1, :, 2 * head :], gs_ref[1], across, preferred_element_type=f32)
    for g in range(2):
        gsg_ref[g] += lax.dot_general(
            low[:, 2 * head :], gg[g, :, 2 * head :], down, preferred_element_type=f32
        )

    def deconvolve(index, sums):
        start = pl.multiple_of(index * 16, 16)
        window = direct[pl.ds(start, 24), :]
        inputs = padded[pl.ds(start, 24), :]
        grad = window[:16]
        out = cw_ref[0:1] * grad
        fold = lambda old, new: old + new[:8] + new[8:]
        new = [fold(sums[0], grad), fold(sums[1], grad * inputs[8:])]
        for k in range(1, taps):
            out = out + cw_ref[k : k + 1] * pltpu.roll(window, 24 - k, 0)[:16]
            new.append(fold(sums[k + 1], grad * pltpu.roll(inputs, k, 0)[8:]))
        gu_ref[0, pl.ds(start, 16), :wide] = out.astype(bf16)
        gu_ref[0, pl.ds(start, 16), wide:] = gy_ref[0, pl.ds(start, 16), :]

        @pl.when(index == tokens // 16 - 1)
        def _():
            tail_ref[0] = out[8:]

        return tuple(new)

    zero = jnp.zeros((8, wide), f32)
    sums = lax.fori_loop(0, tokens // 16, deconvolve, (zero,) * (taps + 1))
    for position, value in enumerate(sums):
        taps_ref[position : position + 1] += jnp.sum(value, axis=0, keepdims=True)
    first = direct[0:8, :]
    row = rows_of((8, wide))
    owed = jnp.zeros((8, wide), f32)
    for k in range(1, taps):
        moved = pltpu.roll(first, 8 - k, 0)
        owed = owed + cw_ref[k : k + 1] * jnp.where(row >= 8 - k, moved, 0.0)
    lead_ref[0] = owed


def mlp_kernel(normed_ref, weight_ref, grad_ref, hidden_ref, out_ref):
    part = hidden_ref.shape[1]
    rows = 512

    def step(index, none):
        span = pl.ds(pl.multiple_of(index * rows, rows), rows)
        both = jnp.dot(normed_ref[span, :], weight_ref[...], preferred_element_type=f32)
        act, slope = gelu_both(both[:, :part])
        up = both[:, part:]
        grad = grad_ref[span, :].astype(f32)
        hidden_ref[span, :] = (act * up).astype(bf16)
        out_ref[span, :part] = (grad * up * slope).astype(bf16)
        out_ref[span, part:] = (grad * act).astype(bf16)
        return none

    lax.fori_loop(0, normed_ref.shape[0] // rows, step, 0)


def spread_mlp_kernel(layout, mine_ref, a_ref, b_ref, c_ref, d_ref, out_ref):
    parts, per_part, fine = layout
    blocks = (a_ref, b_ref, c_ref, d_ref)
    part = per_part * fine
    span = part * len(blocks)
    for mine in range(len(blocks)):

        @pl.when(mine_ref[0] == mine)
        def _(mine=mine):
            for p in range(parts):
                for h in range(2):
                    base = (2 * p + h) * part
                    wholes = [blocks[k][:, base : base + part].astype(f32) for k in range(len(blocks))]
                    pieces = [
                        wholes[mine ^ a][:, g * fine : (g + 1) * fine]
                        for g in range(per_part)
                        for a in range(len(blocks))
                    ]
                    at = (h * parts + p) * span
                    out_ref[:, at : at + span] = jnp.concatenate(pieces, 1)


def spread_in_kernel(head, mine_ref, a_ref, b_ref, c_ref, d_ref, out_ref):
    blocks = (a_ref, b_ref, c_ref, d_ref)
    half = head // 2
    wide = 3 * head
    rec = out_ref.shape[1] // 2
    for mine in range(len(blocks)):

        @pl.when(mine_ref[0] == mine)
        def _(mine=mine):
            for k, block in enumerate(blocks):
                member = mine ^ k
                first, shared = 5 * (member // 2) + 3 * (member % 2), 5 * (member // 2) + 2
                at = first * head
                out_ref[:, at : at + 2 * head] = block[:, : 2 * head].astype(f32)
                out_ref[:, rec + at : rec + at + 2 * head] = block[:, wide : wide + 2 * head].astype(f32)
                at = rec + shared * head + (member % 2) * half
                out_ref[:, at : at + half] = block[:, wide + 2 * head :].astype(f32)
                if k % 2 == 0:
                    at = shared * head
                    out_ref[:, at : at + head] = block[:, 2 * head : wide].astype(f32) + blocks[k + 1][
                        :, 2 * head : wide
                    ].astype(f32)


def spread(kernel, mine, blocks, columns, name):
    rows, wide = blocks[0].shape
    step = min(32, rows)
    piece = pl.BlockSpec((step, wide), lambda i: (i, 0))
    return pl.pallas_call(
        kernel,
        grid=(rows // step,),
        in_specs=[SCALAR] + [piece] * len(blocks),
        out_specs=pl.BlockSpec((step, columns), lambda i: (i, 0)),
        out_shape=jax.ShapeDtypeStruct((rows, columns), f32),
        compiler_params=params("arbitrary"),
        cost_estimate=cost(8),
        name=name,
    )(mine.astype(jnp.int32).reshape(1), *blocks)


def params(*semantics):
    return pltpu.CompilerParams(dimension_semantics=semantics, vmem_limit_bytes=VMEM_LIMIT)


def per_seq(*shape):
    return pl.BlockSpec((1, *shape), lambda i: (i,) + (0,) * len(shape))


def whole(*shape):
    return pl.BlockSpec(shape, lambda i: (0,) * len(shape))


SCALAR = pl.BlockSpec(memory_space=pltpu.SMEM)


def cost(microseconds):
    return pl.CostEstimate(
        flops=int(microseconds * 1e9), bytes_accessed=int(microseconds * 3e6), transcendentals=0
    )


def shards(
    block_input,
    out_cotangent,
    norm_gain,
    in_weight,
    conv_weight,
    conv_bias,
    gate_weight,
    gate_bias,
    decay_param,
    out_weight,
    mlp_gain,
    mlp_weight,
    down_weight,
):
    _, tokens, model = block_input.shape
    taps, rec = conv_weight.shape
    heads, head = gate_weight.shape[1:3]
    members = lax.axis_size("seq")
    devices = lax.axis_size("group")
    hidden = mlp_weight.shape[1] // 2
    assert members == 4 and heads == 10
    half = head // 2
    own = 2 * head + half
    wide = 3 * head
    mine = lax.axis_index("seq")
    odd = mine % 2

    def first_of(member):
        return 5 * (member // 2) + 3 * (member % 2), 5 * (member // 2) + 2

    first, shared = first_of(mine)

    def widen(value, offset=0):
        return jnp.concatenate(
            [
                lax.dynamic_slice_in_dim(value, offset + first * head, 2 * head, value.ndim - 1),
                lax.dynamic_slice_in_dim(value, offset + shared * head, head, value.ndim - 1),
            ],
            -1,
        )

    def owned(value, offset=0):
        return jnp.concatenate(
            [
                lax.dynamic_slice_in_dim(value, offset + first * head, 2 * head, value.ndim - 1),
                lax.dynamic_slice_in_dim(
                    value, offset + shared * head + odd * half, half, value.ndim - 1
                ),
            ],
            -1,
        )

    in_cols = gather_group(jnp.concatenate([widen(in_weight), owned(in_weight, rec)], 1))
    in_u, in_y = in_cols[:, :wide], in_cols[:, wide:]
    x_own = block_input[0]
    x_blocks = gather_seq(x_own)
    x_all = jnp.concatenate(x_blocks, 0)
    c_own = after(out_cotangent[0], x_blocks[1])
    c_blocks = gather_seq(c_own)
    c_all = jnp.concatenate(c_blocks, 0)
    fine = hidden // devices // members
    part = min(384, hidden // members)
    per_part = part // fine
    parts = hidden // members // part
    cut = after(mlp_weight, x_blocks[1]).reshape(-1, 2, parts, per_part, members, fine)
    cut = lax.dynamic_index_in_dim(cut, mine, 4, keepdims=False)
    cut = cut.transpose(0, 2, 1, 3, 4).reshape(mlp_weight.shape[0], -1)
    normed = after(rms_low(x_all.astype(f32), norm_gain), cut)
    out_piece = model // members
    out_cols = gather_group(
        after(lax.dynamic_slice_in_dim(out_weight, mine * out_piece, out_piece, 1), in_cols, normed)
    )
    def rows_for(value, k):
        start, common = first_of(mine ^ k)
        return jnp.concatenate(
            [
                lax.dynamic_slice_in_dim(value, start * head, 2 * head, 0),
                lax.dynamic_slice_in_dim(
                    value, common * head + ((mine ^ k) % 2) * half, half, 0
                ),
            ],
            0,
        )

    out_rows = jnp.zeros((own, model), bf16)
    for k in range(members):
        piece = rows_for(out_cols, k)
        if k:
            piece = swap(piece, k)
        out_rows = lax.dynamic_update_slice_in_dim(out_rows, piece, (mine ^ k) * out_piece, 1)

    u = jnp.dot(normed, in_u, preferred_element_type=f32).reshape(members, tokens, wide)
    u = after(u, c_blocks[1], c_blocks[2])
    y = jnp.dot(normed, in_y, preferred_element_type=f32).reshape(members, tokens, own)
    lead = taps - 1
    rim = jnp.pad(shift(u[:, tokens - lead :], 1), ((0, 0), (8 - lead, 0), (0, 0)))
    odd_flag = odd.astype(jnp.int32).reshape(1)
    cw = widen(conv_weight)
    cb = widen(conv_bias)[None]
    gb = owned(gate_bias)
    soft = -8.0 * owned(jax.nn.softplus(decay_param))[None]
    gw = lax.dynamic_slice_in_dim(gate_weight, first, 2, 1)
    gs = lax.dynamic_slice(
        gate_weight, (0, shared, 0, odd * half), (2, 1, head, half)
    )[:, 0]
    rows = members * tokens
    full = jax.ShapeDtypeStruct((members, tokens, own), f32)
    conv, recur, gate, decay, state_local, decay_cum = pl.pallas_call(
        functools.partial(forward_kernel, head),
        grid=(members,),
        in_specs=[
            SCALAR,
            per_seq(tokens, wide),
            per_seq(8, wide),
            whole(taps, wide),
            whole(1, wide),
            whole(2, 2, head, head),
            whole(2, head, half),
            whole(2, own),
            whole(1, own),
        ],
        out_specs=[per_seq(tokens, wide)] + [per_seq(tokens, own)] * 5,
        out_shape=[jax.ShapeDtypeStruct((members, tokens, wide), f32)] + [full] * 5,
        scratch_shapes=[
            pltpu.VMEM((tokens + 8, wide), f32),
            pltpu.VMEM((tokens, wide), bf16),
            pltpu.VMEM((2, tokens, own), f32),
        ],
        compiler_params=params("arbitrary"),
        cost_estimate=cost(14),
        name="recurrence_forward",
    )(odd_flag, u, rim, cw, cb, gw, gs, gb, soft)
    down_rows = gather_group(
        after(
            lax.dynamic_slice_in_dim(down_weight, mine * fine, fine, 0), out_cols, u
        )
    )
    carried = entering(decay_cum[:, -1], state_local[:, -1], 1)
    arrived = carried
    carried = after(carried, out_rows)
    carried8 = jnp.broadcast_to(carried[:, None], (members, 8, own))
    h, merged = pl.pallas_call(
        merge_kernel,
        grid=(members,),
        in_specs=[per_seq(tokens, own)] * 2 + [per_seq(8, own), per_seq(tokens, own)],
        out_specs=[per_seq(tokens, own)] * 2,
        out_shape=[full, jax.ShapeDtypeStruct((members, tokens, own), bf16)],
        compiler_params=params("arbitrary"),
        cost_estimate=cost(14),
        name="recurrence_merge",
    )(state_local, decay_cum, carried8, y)
    partial = jnp.dot(merged.reshape(rows, own), out_rows, preferred_element_type=f32)
    partial = partial.astype(bf16)
    mlp_cols = gather_group(after(cut, down_rows, out_rows, arrived))
    partial = lax.optimization_barrier(partial).reshape(members, tokens, model)
    x32 = x_own.astype(f32)
    grad_hidden = lax.dot_general(
        c_all, down_rows, (((1,), (1,)), ((), ())), preferred_element_type=f32
    )
    resid = after(x32 + scatter_seq(partial), grad_hidden)
    normed2 = jnp.concatenate(gather_seq(rms_low(resid, mlp_gain)), 0)

    width = parts * part
    hidden_low, grad_gu = pl.pallas_call(
        mlp_kernel,
        grid=(parts,),
        in_specs=[
            whole(rows, model),
            pl.BlockSpec((model, 2 * part), lambda i: (0, i)),
            pl.BlockSpec((rows, part), lambda i: (0, i)),
        ],
        out_specs=[
            pl.BlockSpec((rows, part), lambda i: (0, i)),
            pl.BlockSpec((rows, 2 * part), lambda i: (0, i)),
        ],
        out_shape=[
            jax.ShapeDtypeStruct((rows, width), bf16),
            jax.ShapeDtypeStruct((rows, 2 * width), bf16),
        ],
        compiler_params=params("arbitrary"),
        cost_estimate=pl.CostEstimate(
            flops=4 * rows * model * width,
            bytes_accessed=rows * model * 2 + model * width * 4 + rows * width * 10,
            transcendentals=rows * width,
        ),
        name="mlp",
    )(normed2, mlp_cols, grad_hidden)
    across = (((1,), (1,)), ((), ()))
    down = (((0,), (0,)), ((), ()))
    down_part = lax.dot_general(hidden_low, c_all, down, preferred_element_type=f32).astype(bf16)
    down_sum = scatter_group(down_part)
    partial = lax.dot_general(
        after(grad_gu, down_part), mlp_cols, across, preferred_element_type=f32
    ).astype(bf16)
    mlp_part = lax.dot_general(
        normed2, after(grad_gu, partial), down, preferred_element_type=f32
    ).astype(bf16)
    grad_normed2 = scatter_seq(lax.optimization_barrier(partial).reshape(members, tokens, model))
    final = jnp.dot(
        after(hidden_low, mlp_part), down_rows, preferred_element_type=f32
    ).astype(bf16)
    grad_normed2 = after(grad_normed2, final)
    grad_resid_norm, mlp_gain_grad = rms_back(resid, mlp_gain, grad_normed2)
    grad_resid = c_own.astype(f32) + grad_resid_norm
    grad_resid_all = jnp.concatenate(gather_seq(grad_resid.astype(bf16)), 0)
    mlp_sum = scatter_group(after(mlp_part, down_sum, grad_normed2))

    final = after(final, grad_resid_all).reshape(members, tokens, model)
    final_hop = first_hop(final[3])
    block_out = (resid + scatter_seq(final, final_hop)).astype(bf16)[None]
    grad_merged = lax.dot_general(
        grad_resid_all, out_rows, (((1,), (1,)), ((), ())), preferred_element_type=f32
    ).reshape(members, tokens, own)
    grad_merged = after(grad_merged, *final_hop)
    down_first = after(down_sum, *final_hop)
    down_hop = swap(down_first, 1), swap(down_first, 2)
    grad_h, grad_y, back_local, back_cum = pl.pallas_call(
        adjoint_kernel,
        grid=(members,),
        in_specs=[per_seq(tokens, own)] * 4,
        out_specs=[per_seq(tokens, own)] * 4,
        out_shape=[full, jax.ShapeDtypeStruct((members, tokens, own), bf16), full, full],
        compiler_params=params("arbitrary"),
        cost_estimate=cost(10),
        name="recurrence_adjoint",
    )(grad_merged, h, y, decay)
    incoming = entering(back_cum[:, 0], back_local[:, 0], -1)
    incoming = after(incoming, block_out)
    incoming8 = jnp.broadcast_to(incoming[:, None], (members, 8, own))
    grad_proj, tail, owed, small, tap_sums, gw_grad, gs_grad = pl.pallas_call(
        functools.partial(backward_kernel, head),
        grid=(members,),
        in_specs=[
            SCALAR,
            *[per_seq(tokens, own)] * 4,
            per_seq(8, own),
            per_seq(8, own),
            *[per_seq(tokens, own)] * 3,
            *[per_seq(tokens, wide)] * 2,
            per_seq(tokens, own),
            per_seq(8, wide),
            whole(taps, wide),
            whole(2, 2, head, head),
            whole(2, head, half),
            whole(1, own),
        ],
        out_specs=[
            per_seq(tokens, wide + own),
            per_seq(8, wide),
            per_seq(8, wide),
            whole(8, own),
            whole(8, wide),
            whole(2, 2, head, head),
            whole(2, head, half),
        ],
        out_shape=[
            jax.ShapeDtypeStruct((members, tokens, wide + own), bf16),
            jax.ShapeDtypeStruct((members, 8, wide), f32),
            jax.ShapeDtypeStruct((members, 8, wide), f32),
            jax.ShapeDtypeStruct((8, own), f32),
            jax.ShapeDtypeStruct((8, wide), f32),
            jax.ShapeDtypeStruct((2, 2, head, head), f32),
            jax.ShapeDtypeStruct((2, head, half), f32),
        ],
        scratch_shapes=[
            pltpu.VMEM((tokens + 8, wide), f32),
            pltpu.VMEM((tokens + 8, own), f32),
            pltpu.VMEM((tokens + 8, own), f32),
            pltpu.VMEM((tokens, wide), bf16),
            pltpu.VMEM((2, tokens, own), bf16),
            pltpu.VMEM((tokens + 8, wide), f32),
        ],
        compiler_params=params("arbitrary"),
        cost_estimate=cost(19),
        name="recurrence_backward",
    )(
        odd_flag, back_local, back_cum, grad_h, h, carried8, incoming8, recur, gate,
        decay, conv, u, grad_y, rim, cw, gw, gs, soft,
    )
    tail = (tail + shift(owed, -1)).astype(bf16)
    grad_proj = lax.dynamic_update_slice(grad_proj, tail, (0, tokens - 8, 0))
    grad_proj = grad_proj.reshape(rows, wide + own)
    out_part = lax.dot_general(
        merged.reshape(rows, own), grad_resid_all, down, preferred_element_type=f32
    ).astype(bf16)
    pieces = []
    for k in range(members):
        piece = lax.dynamic_slice_in_dim(out_part, (mine ^ k) * out_piece, out_piece, 1)
        pieces.append(swap(piece, k) if k else piece)
    pieces = jnp.stack(pieces)
    out_terms = []
    for member in range(members):
        piece = lax.dynamic_index_in_dim(pieces, mine ^ member, 0, keepdims=False)
        cut_at = 2 * head if member % 2 else 0
        out_terms += [piece[cut_at:], piece[:cut_at]]
    out_terms = jnp.concatenate(out_terms, 0)
    gate_terms = jnp.concatenate([gw_grad[:, 0], gw_grad[:, 1], gs_grad], -1).reshape(-1, own)
    decay_terms = small[2:3] * (-8.0) * owned(jax.nn.sigmoid(decay_param))[None]
    sizes = ((taps + 1) * wide, 3 * own, model)
    small_terms = jnp.concatenate(
        [
            tap_sums[: taps + 1].reshape(-1),
            small[:2].reshape(-1),
            decay_terms.reshape(-1),
            mlp_gain_grad,
        ]
    )
    small_rows = 64
    small_terms = jnp.pad(small_terms, (0, small_rows * own - small_terms.shape[0]))
    terms = jnp.concatenate([gate_terms, small_terms.reshape(small_rows, own)], 0).astype(bf16)
    group_terms = total_group(terms)
    partial = lax.dot_general(
        after(grad_proj, out_terms, *down_hop, group_terms), in_cols, across, preferred_element_type=f32
    )
    partial = lax.optimization_barrier(partial.astype(bf16)).reshape(members, tokens, model)
    hop = first_hop(partial[3])
    out_sum = scatter_group(after(out_terms, mlp_sum, grad_proj))
    mlp_hop = swap(mlp_sum, 1), swap(mlp_sum, 2)
    in_part = lax.dot_general(normed, grad_proj, down, preferred_element_type=f32).astype(bf16)
    in_sum = scatter_group(after(in_part, out_sum, *hop, *mlp_hop))

    out_blocks = gather_seq(out_sum)
    grad_normed = scatter_seq(partial, (after(hop[0], out_sum), after(hop[1], out_sum)))
    term_parts = gather_seq(after(group_terms, grad_normed))
    gate_parts = [after(piece[: 2 * head], in_sum) for piece in term_parts]
    small_parts = jnp.stack(
        [after(piece[2 * head :], in_sum).reshape(-1) for piece in term_parts]
    )
    mlp_blocks = gather_seq(mlp_sum, mlp_hop)
    grad_input_norm, norm_gain_grad = rms_back(x32, norm_gain, grad_normed)
    input_grad = (grad_resid + grad_input_norm)[None]

    mlp_grad = spread(
        functools.partial(spread_mlp_kernel, (parts, per_part, fine)),
        mine,
        mlp_blocks,
        2 * hidden,
        "spread_mlp",
    )
    out_parts = jnp.stack(out_blocks)
    out_grad = jnp.concatenate(
        [lax.dynamic_index_in_dim(out_parts, mine ^ a, 0, keepdims=False) for a in range(members)],
        1,
    ).astype(f32)
    down_parts = jnp.stack(gather_seq(down_sum, down_hop))
    down_grad = jnp.concatenate(
        [lax.dynamic_index_in_dim(down_parts, mine ^ a, 0, keepdims=False) for a in range(members)],
        0,
    ).astype(f32)
    gate_grad = jnp.zeros((2, heads, head, head), f32)
    for k in range(members):
        start, common = first_of(mine ^ k)
        block = gate_parts[k].reshape(2, head, own).astype(f32)
        pair = block[:, :, : 2 * head].reshape(2, head, 2, head).transpose(0, 2, 1, 3)
        gate_grad = lax.dynamic_update_slice_in_dim(gate_grad, pair, start, 1)
        if k % 2 == 0:
            other = gate_parts[k + 1].reshape(2, head, own).astype(f32)
            halves = jnp.where(
                odd == 1,
                jnp.concatenate([other[..., 2 * head :], block[..., 2 * head :]], -1),
                jnp.concatenate([block[..., 2 * head :], other[..., 2 * head :]], -1),
            )
            gate_grad = lax.dynamic_update_slice_in_dim(gate_grad, halves[:, None], common, 1)

    def place(value, member, wide_shared):
        start, common = first_of(member)
        at = common * head if wide_shared else common * head + (member % 2) * half
        out = jnp.zeros((value.shape[0], rec), f32)
        out = lax.dynamic_update_slice_in_dim(out, value[:, : 2 * head], start * head, 1)
        return lax.dynamic_update_slice_in_dim(out, value[:, 2 * head :], at, 1)

    tap_grads, own_grads, mlp_gain_grad = 0.0, 0.0, 0.0
    for member in range(members):
        piece = lax.dynamic_index_in_dim(small_parts, mine ^ member, 0, keepdims=False).astype(f32)
        one, two, three, _ = jnp.split(
            piece, (sizes[0], sizes[0] + sizes[1], sizes[0] + sizes[1] + sizes[2])
        )
        tap_grads = tap_grads + place(one.reshape(-1, wide), member, True)
        own_grads = own_grads + place(two.reshape(-1, own), member, False)
        mlp_gain_grad = mlp_gain_grad + three
    norm_gain_grad = total(norm_gain_grad.reshape(-1, 128)).reshape(-1)
    in_grad = spread(
        functools.partial(spread_in_kernel, head), mine, gather_seq(after(in_sum, *mlp_hop, *out_blocks, *term_parts)), 2 * rec, "spread_in"
    )

    return (
        block_out,
        input_grad,
        norm_gain_grad,
        in_grad,
        tap_grads[1:],
        tap_grads[0],
        gate_grad,
        own_grads[:2],
        own_grads[2],
        out_grad,
        mlp_gain_grad,
        mlp_grad,
        down_grad,
    )


def solution(mesh):
    tokens = P("seq", "group", None)
    rows = P("group", None)
    in_specs = (tokens, tokens, P(), rows, P(), P(), P(), P(), P(), rows, P(), rows, rows)
    out_specs = (tokens, tokens, P(), rows, P(), P(), P(), P(), P(), rows, P(), rows, rows)
    return jax.shard_map(shards, mesh=mesh, in_specs=in_specs, out_specs=out_specs, check_vma=False)
```

```python
import functools

import jax
import jax.numpy as jnp
from jax import lax
from jax.experimental import pallas as pl
from jax.experimental.pallas import tpu as pltpu
from jax.sharding import PartitionSpec as P

epsilon = 1e-06
f32 = jnp.float32
bf16 = jnp.bfloat16
VMEM_LIMIT = 58 * 1024 * 1024


def swap(block, k):
    return lax.ppermute(block, "seq", [(i, i ^ k) for i in range(lax.axis_size("seq"))])


def shift(block, distance):
    devices = range(lax.axis_size("group"))
    return lax.ppermute(
        block, "group", [(i - distance, i) for i in devices if i - distance in devices]
    )


def gather_seq(block, hop=None):
    half = block.shape[0] // 2
    first, second = (swap(block, 1), swap(block, 2)) if hop is None else hop
    third = jnp.concatenate([swap(first[:half], 2), swap(second[half:], 1)], 0)
    return [block, first, second, third]


def first_hop(third):
    half = third.shape[0] // 2
    return swap(third[:half], 1), swap(third[half:], 2)


def scatter_seq(parts, hop=None):
    half = parts[0].shape[0] // 2
    own, first, second, third = parts
    top, bottom = first_hop(third) if hop is None else hop
    first_top = swap(first[:half], 1)
    second_bottom = swap(second[half:], 2)
    second_top = swap((second[:half].astype(f32) + top.astype(f32)).astype(bf16), 2)
    first_bottom = swap((first[half:].astype(f32) + bottom.astype(f32)).astype(bf16), 1)
    return jnp.concatenate(
        [
            own[:half].astype(f32) + first_top.astype(f32) + second_top.astype(f32),
            own[half:].astype(f32) + first_bottom.astype(f32) + second_bottom.astype(f32),
        ],
        0,
    )


def gather_group(block):
    return lax.all_gather(block, "group", axis=0, tiled=True)


def scatter_group(block):
    return lax.psum_scatter(block, "group", scatter_dimension=0, tiled=True)


def after(value, *others):
    return lax.optimization_barrier((value, *others))[0]


def total_group(value):
    count = lax.axis_size("group")
    place = lax.axis_index("group")
    route = lambda step: [(i, i ^ step) for i in range(count)]
    steps = [1 << i for i in range(count.bit_length() - 1)]
    for step in steps:
        half = value.shape[0] // 2
        bit = (place // step) % 2
        kept = lax.dynamic_slice_in_dim(value, bit * half, half, 0)
        given = lax.dynamic_slice_in_dim(value, (1 - bit) * half, half, 0)
        got = lax.ppermute(given, "group", route(step))
        value = (kept.astype(f32) + got.astype(f32)).astype(value.dtype)
    for step in reversed(steps):
        bit = (place // step) % 2
        got = lax.ppermute(value, "group", route(step))
        value = jnp.where(
            bit == 0, jnp.concatenate([value, got], 0), jnp.concatenate([got, value], 0)
        )
    return value


def total(value):
    for axis in ("group", "seq"):
        count = lax.axis_size(axis)
        step = 1
        while step < count:
            value = value + lax.ppermute(value, axis, [(i, i ^ step) for i in range(count)])
            step *= 2
    return value


def link(earlier, later):
    return (earlier[0] * later[0], later[1] + later[0] * earlier[1])


def entering(decay, state, sign):
    count = lax.axis_size("group")
    pair = jnp.stack([decay, state])
    near = [shift(pair, sign * distance) for distance in range(1, min(4, count - 1) + 1)]
    decay, state = near[0][0], near[0][1]
    for before in near[1:]:
        decay, state = link((before[0], before[1]), (decay, state))
    covered = len(near)
    while covered < count - 1:
        before = shift(jnp.stack([decay, state]), sign * covered)
        decay, state = link((before[0], before[1]), (decay, state))
        covered *= 2
    return state


def rms_low(value, gain):
    scale = lax.rsqrt(jnp.mean(value * value, axis=-1, keepdims=True) + epsilon)
    return (value * scale * gain).astype(bf16)


def rms_back(value, gain, grad):
    width = value.shape[-1]
    scale = lax.rsqrt(jnp.mean(value * value, axis=-1, keepdims=True) + epsilon)
    scaled = grad * gain
    along = jnp.sum(scaled * value, axis=-1, keepdims=True) / width
    grad_value = scale * scaled - value * (scale * scale * scale * along)
    grad_gain = jnp.sum(grad * value * scale, axis=0)
    return grad_value, grad_gain


ROOT = 0.7978845608028654
CUBE = 0.044715


def gelu(v):
    return 0.5 * v * (1.0 + jnp.tanh(ROOT * (v + CUBE * v * v * v)))


def gelu_both(v):
    square = v * v
    t = jnp.tanh(ROOT * v * (1.0 + CUBE * square))
    half = 0.5 * (1.0 + t)
    slope = half + 0.5 * v * (1.0 - t * t) * (ROOT * (1.0 + 3.0 * CUBE * square))
    return v * half, slope


def one_less_square(double):
    series = jnp.full_like(double, 1.0 / 362880.0)
    for term in (40320.0, 5040.0, 720.0, 120.0, 24.0, 6.0, 2.0, 1.0):
        series = series * double + 1.0 / term
    return -double * series


def rows_of(shape):
    return lax.broadcasted_iota(jnp.int32, shape, 0)


def pick(odd, value, width):
    lanes = value.shape[-1]
    return jnp.where(odd, value[:, lanes - width :], value[:, lanes - 2 * width : lanes - width])


def forward_kernel(
    head, odd_ref, u_ref, rim_ref, cw_ref, cb_ref, gw_ref, gs_ref, gb_ref, sp_ref,
    conv_ref, recur_ref, input_ref, decay_ref, state_ref, cum_ref,
    padded, low, pre,
):
    tokens, wide = u_ref.shape[1:]
    own = recur_ref.shape[2]
    odd = odd_ref[0] == 1
    padded[0:8] = rim_ref[0]
    padded[8:] = u_ref[0]
    taps = cw_ref.shape[0]

    def convolve(index, carry):
        start = pl.multiple_of(index * 32, 32)
        window = padded[pl.ds(start, 40), :]
        out = cb_ref[...] + cw_ref[0:1] * window[8:]
        for k in range(1, taps):
            out = out + cw_ref[k : k + 1] * pltpu.roll(window, k, 0)[8:]
        conv_ref[0, pl.ds(start, 32), :] = out
        low[pl.ds(start, 32), :] = out.astype(bf16)
        return carry

    lax.fori_loop(0, tokens // 32, convolve, 0)
    for g in range(2):
        for h in range(2):
            cols = slice(h * head, (h + 1) * head)
            pre[g, :, cols] = jnp.dot(low[:, cols], gw_ref[g, h], preferred_element_type=f32)
        pre[g, :, 2 * head :] = jnp.dot(low[:, 2 * head :], gs_ref[g], preferred_element_type=f32)
    row = rows_of((8, own))

    def scan(index, carry):
        cum, state = carry
        start = pl.multiple_of(index * 16, 16)
        span = pl.ds(start, 16)
        recur = jax.nn.sigmoid(pre[0, span, :] + gb_ref[0:1])
        gate = jax.nn.sigmoid(pre[1, span, :] + gb_ref[1:2])
        log_decay = recur * sp_ref[...]
        decay = jnp.exp(log_decay)
        conv = conv_ref[0, span, :]
        conv = jnp.concatenate([conv[:, : 2 * head], pick(odd, conv, head // 2)], 1)
        driven = conv * gate * jnp.sqrt(one_less_square(2.0 * log_decay))
        recur_ref[0, span, :] = recur
        input_ref[0, span, :] = gate
        decay_ref[0, span, :] = decay
        for tile in range(2):
            a = decay[tile * 8 : tile * 8 + 8]
            b = driven[tile * 8 : tile * 8 + 8]
            for d in (1, 2, 4):
                there = row >= d
                before_a = jnp.where(there, pltpu.roll(a, d, 0), 1.0)
                before_b = jnp.where(there, pltpu.roll(b, d, 0), 0.0)
                b = b + a * before_b
                a = a * before_a
            b = b + a * state
            a = a * cum
            place = pl.ds(start + tile * 8, 8)
            state_ref[0, place, :] = b
            cum_ref[0, place, :] = a
            cum, state = a[7:8], b[7:8]
        return cum, state

    lax.fori_loop(
        0, tokens // 16, scan, (jnp.ones((1, own), f32), jnp.zeros((1, own), f32))
    )


def merge_kernel(state_ref, cum_ref, carry_ref, pre_ref, h_ref, merged_ref):
    def step(index, none):
        span = pl.ds(pl.multiple_of(index * 32, 32), 32)
        state = state_ref[0, span, :] + cum_ref[0, span, :] * carry_ref[0, 0:1]
        h_ref[0, span, :] = state
        merged_ref[0, span, :] = (state * gelu(pre_ref[0, span, :])).astype(bf16)
        return none

    lax.fori_loop(0, state_ref.shape[1] // 32, step, 0)


def adjoint_kernel(gm_ref, h_ref, pre_ref, decay_ref, gh_ref, gpre_ref, back_ref, cum_ref):
    tokens, own = gm_ref.shape[1:]
    row = rows_of((8, own))
    count = tokens // 16

    def step(index, carry):
        cum, back = carry
        start = pl.multiple_of((count - 1 - index) * 16, 16)
        span = pl.ds(start, 16)
        grad = gm_ref[0, span, :]
        act, slope = gelu_both(pre_ref[0, span, :])
        gpre_ref[0, span, :] = (grad * h_ref[0, span, :] * slope).astype(bf16)
        grad_h = grad * act
        gh_ref[0, span, :] = grad_h
        decay = decay_ref[0, span, :]
        driven = decay * grad_h
        for tile in (1, 0):
            a = decay[tile * 8 : tile * 8 + 8]
            b = driven[tile * 8 : tile * 8 + 8]
            for d in (1, 2, 4):
                there = row < 8 - d
                after_a = jnp.where(there, pltpu.roll(a, 8 - d, 0), 1.0)
                after_b = jnp.where(there, pltpu.roll(b, 8 - d, 0), 0.0)
                b = b + a * after_b
                a = a * after_a
            b = b + a * back
            a = a * cum
            place = pl.ds(start + tile * 8, 8)
            back_ref[0, place, :] = b
            cum_ref[0, place, :] = a
            cum, back = a[0:1], b[0:1]
        return cum, back

    lax.fori_loop(0, count, step, (jnp.ones((1, own), f32), jnp.zeros((1, own), f32)))


def backward_kernel(
    head, odd_ref, back_ref, cum_ref, gh_ref, h_ref, carry_ref, enter_ref, recur_ref, input_ref,
    decay_ref, conv_ref, u_ref, gy_ref, rim_ref, cw_ref, gw_ref, gs_ref, sp_ref,
    gu_ref, tail_ref, lead_ref, small_ref, taps_ref, gwg_ref, gsg_ref,
    padded, ahead, behind, low, gg, direct,
):
    tokens, wide = u_ref.shape[1:]
    own = recur_ref.shape[2]
    half = head // 2
    odd = odd_ref[0] == 1
    taps = cw_ref.shape[0]

    @pl.when(pl.program_id(0) == 0)
    def _():
        small_ref[...] = jnp.zeros_like(small_ref)
        taps_ref[...] = jnp.zeros_like(taps_ref)
        gwg_ref[...] = jnp.zeros_like(gwg_ref)
        gsg_ref[...] = jnp.zeros_like(gsg_ref)

    padded[0:8] = rim_ref[0]
    padded[8:] = u_ref[0]
    behind[0:8] = carry_ref[0]
    ahead[tokens:] = enter_ref[0]
    direct[tokens:] = jnp.zeros((8, wide), f32)
    enter = enter_ref[0, 0:1]

    def prepare(index, none):
        start = pl.multiple_of(index * 32, 32)
        span = pl.ds(start, 32)
        ahead[span, :] = back_ref[0, span, :] + cum_ref[0, span, :] * enter
        behind[pl.ds(start + 8, 32), :] = h_ref[0, span, :]
        return none

    lax.fori_loop(0, tokens // 32, prepare, 0)

    def gates(index, sums):
        sum_recur, sum_input, sum_decay = sums
        start = pl.multiple_of(index * 16, 16)
        span = pl.ds(start, 16)
        after = pltpu.roll(ahead[pl.ds(start, 24), :], 23, 0)[:16]
        before = pltpu.roll(behind[pl.ds(start, 24), :], 1, 0)[8:]
        adj = gh_ref[0, span, :] + after
        recur = recur_ref[0, span, :]
        gate = input_ref[0, span, :]
        decay = decay_ref[0, span, :]
        whole = conv_ref[0, span, :]
        low[span, :] = whole.astype(bf16)
        conv = jnp.concatenate([whole[:, : 2 * head], pick(odd, whole, half)], 1)
        square = one_less_square(2.0 * (recur * sp_ref[...]))
        inverse = lax.rsqrt(square)
        root = square * inverse
        grad_a = adj * before
        part = adj * gate
        grad_direct = part * root
        grad_gate = adj * conv * root
        grad_root = part * conv
        grad_log = decay * (grad_a - grad_root * decay * inverse)
        scaled = grad_log * recur
        grad_recur = scaled * sp_ref[...] * (1.0 - recur)
        grad_input = grad_gate * gate * (1.0 - gate)
        gg[0, span, :] = grad_recur.astype(bf16)
        gg[1, span, :] = grad_input.astype(bf16)
        shared = grad_direct[:, 2 * head :]
        none = jnp.zeros_like(shared)
        direct[span, :] = jnp.concatenate(
            [grad_direct[:, : 2 * head], jnp.where(odd, none, shared), jnp.where(odd, shared, none)],
            1,
        )
        fold = lambda old, new: old + new[:8] + new[8:]
        return fold(sum_recur, grad_recur), fold(sum_input, grad_input), fold(sum_decay, scaled)

    zero = jnp.zeros((8, own), f32)
    sums = lax.fori_loop(0, tokens // 16, gates, (zero, zero, zero))
    for position, value in enumerate(sums):
        small_ref[position : position + 1] += jnp.sum(value, axis=0, keepdims=True)
    across = (((1,), (1,)), ((), ()))
    down = (((0,), (0,)), ((), ()))
    for h in range(2):
        cols = slice(h * head, (h + 1) * head)
        direct[0:tokens, cols] += lax.dot_general(
            gg[0, :, cols], gw_ref[0, h], across, preferred_element_type=f32
        ) + lax.dot_general(gg[1, :, cols], gw_ref[1, h], across, preferred_element_type=f32)
        for g in range(2):
            gwg_ref[g, h] += lax.dot_general(
                low[:, cols], gg[g, :, cols], down, preferred_element_type=f32
            )
    direct[0:tokens, 2 * head :] += lax.dot_general(
        gg[0, :, 2 * head :], gs_ref[0], across, preferred_element_type=f32
    ) + lax.dot_general(gg[1, :, 2 * head :], gs_ref[1], across, preferred_element_type=f32)
    for g in range(2):
        gsg_ref[g] += lax.dot_general(
            low[:, 2 * head :], gg[g, :, 2 * head :], down, preferred_element_type=f32
        )

    def deconvolve(index, sums):
        start = pl.multiple_of(index * 16, 16)
        window = direct[pl.ds(start, 24), :]
        inputs = padded[pl.ds(start, 24), :]
        grad = window[:16]
        out = cw_ref[0:1] * grad
        fold = lambda old, new: old + new[:8] + new[8:]
        new = [fold(sums[0], grad), fold(sums[1], grad * inputs[8:])]
        for k in range(1, taps):
            out = out + cw_ref[k : k + 1] * pltpu.roll(window, 24 - k, 0)[:16]
            new.append(fold(sums[k + 1], grad * pltpu.roll(inputs, k, 0)[8:]))
        gu_ref[0, pl.ds(start, 16), :wide] = out.astype(bf16)
        gu_ref[0, pl.ds(start, 16), wide:] = gy_ref[0, pl.ds(start, 16), :]

        @pl.when(index == tokens // 16 - 1)
        def _():
            tail_ref[0] = out[8:]

        return tuple(new)

    zero = jnp.zeros((8, wide), f32)
    sums = lax.fori_loop(0, tokens // 16, deconvolve, (zero,) * (taps + 1))
    for position, value in enumerate(sums):
        taps_ref[position : position + 1] += jnp.sum(value, axis=0, keepdims=True)
    first = direct[0:8, :]
    row = rows_of((8, wide))
    owed = jnp.zeros((8, wide), f32)
    for k in range(1, taps):
        moved = pltpu.roll(first, 8 - k, 0)
        owed = owed + cw_ref[k : k + 1] * jnp.where(row >= 8 - k, moved, 0.0)
    lead_ref[0] = owed


def mlp_kernel(normed_ref, weight_ref, grad_ref, hidden_ref, out_ref):
    part = hidden_ref.shape[1]
    rows = 512

    def step(index, none):
        span = pl.ds(pl.multiple_of(index * rows, rows), rows)
        both = jnp.dot(normed_ref[span, :], weight_ref[...], preferred_element_type=f32)
        act, slope = gelu_both(both[:, :part])
        up = both[:, part:]
        grad = grad_ref[span, :].astype(f32)
        hidden_ref[span, :] = (act * up).astype(bf16)
        out_ref[span, :part] = (grad * up * slope).astype(bf16)
        out_ref[span, part:] = (grad * act).astype(bf16)
        return none

    lax.fori_loop(0, normed_ref.shape[0] // rows, step, 0)


def spread_mlp_kernel(layout, mine_ref, a_ref, b_ref, c_ref, d_ref, out_ref):
    parts, per_part, fine = layout
    blocks = (a_ref, b_ref, c_ref, d_ref)
    part = per_part * fine
    span = part * len(blocks)
    for mine in range(len(blocks)):

        @pl.when(mine_ref[0] == mine)
        def _(mine=mine):
            for p in range(parts):
                for h in range(2):
                    base = (2 * p + h) * part
                    wholes = [blocks[k][:, base : base + part].astype(f32) for k in range(len(blocks))]
                    pieces = [
                        wholes[mine ^ a][:, g * fine : (g + 1) * fine]
                        for g in range(per_part)
                        for a in range(len(blocks))
                    ]
                    at = (h * parts + p) * span
                    out_ref[:, at : at + span] = jnp.concatenate(pieces, 1)


def spread_in_kernel(head, mine_ref, a_ref, b_ref, c_ref, d_ref, out_ref):
    blocks = (a_ref, b_ref, c_ref, d_ref)
    half = head // 2
    wide = 3 * head
    rec = out_ref.shape[1] // 2
    for mine in range(len(blocks)):

        @pl.when(mine_ref[0] == mine)
        def _(mine=mine):
            for k, block in enumerate(blocks):
                member = mine ^ k
                first, shared = 5 * (member // 2) + 3 * (member % 2), 5 * (member // 2) + 2
                at = first * head
                out_ref[:, at : at + 2 * head] = block[:, : 2 * head].astype(f32)
                out_ref[:, rec + at : rec + at + 2 * head] = block[:, wide : wide + 2 * head].astype(f32)
                at = rec + shared * head + (member % 2) * half
                out_ref[:, at : at + half] = block[:, wide + 2 * head :].astype(f32)
                if k % 2 == 0:
                    at = shared * head
                    out_ref[:, at : at + head] = block[:, 2 * head : wide].astype(f32) + blocks[k + 1][
                        :, 2 * head : wide
                    ].astype(f32)


def spread(kernel, mine, blocks, columns, name):
    rows, wide = blocks[0].shape
    step = min(32, rows)
    piece = pl.BlockSpec((step, wide), lambda i: (i, 0))
    return pl.pallas_call(
        kernel,
        grid=(rows // step,),
        in_specs=[SCALAR] + [piece] * len(blocks),
        out_specs=pl.BlockSpec((step, columns), lambda i: (i, 0)),
        out_shape=jax.ShapeDtypeStruct((rows, columns), f32),
        compiler_params=params("arbitrary"),
        cost_estimate=cost(8),
        name=name,
    )(mine.astype(jnp.int32).reshape(1), *blocks)


def params(*semantics):
    return pltpu.CompilerParams(dimension_semantics=semantics, vmem_limit_bytes=VMEM_LIMIT)


def per_seq(*shape):
    return pl.BlockSpec((1, *shape), lambda i: (i,) + (0,) * len(shape))


def whole(*shape):
    return pl.BlockSpec(shape, lambda i: (0,) * len(shape))


SCALAR = pl.BlockSpec(memory_space=pltpu.SMEM)


def cost(microseconds):
    return pl.CostEstimate(
        flops=int(microseconds * 1e9), bytes_accessed=int(microseconds * 3e6), transcendentals=0
    )


def shards(
    block_input,
    out_cotangent,
    norm_gain,
    in_weight,
    conv_weight,
    conv_bias,
    gate_weight,
    gate_bias,
    decay_param,
    out_weight,
    mlp_gain,
    mlp_weight,
    down_weight,
):
    _, tokens, model = block_input.shape
    taps, rec = conv_weight.shape
    heads, head = gate_weight.shape[1:3]
    members = lax.axis_size("seq")
    devices = lax.axis_size("group")
    hidden = mlp_weight.shape[1] // 2
    assert members == 4 and heads == 10
    half = head // 2
    own = 2 * head + half
    wide = 3 * head
    mine = lax.axis_index("seq")
    odd = mine % 2

    def first_of(member):
        return 5 * (member // 2) + 3 * (member % 2), 5 * (member // 2) + 2

    first, shared = first_of(mine)

    def widen(value, offset=0):
        return jnp.concatenate(
            [
                lax.dynamic_slice_in_dim(value, offset + first * head, 2 * head, value.ndim - 1),
                lax.dynamic_slice_in_dim(value, offset + shared * head, head, value.ndim - 1),
            ],
            -1,
        )

    def owned(value, offset=0):
        return jnp.concatenate(
            [
                lax.dynamic_slice_in_dim(value, offset + first * head, 2 * head, value.ndim - 1),
                lax.dynamic_slice_in_dim(
                    value, offset + shared * head + odd * half, half, value.ndim - 1
                ),
            ],
            -1,
        )

    in_cols = gather_group(jnp.concatenate([widen(in_weight), owned(in_weight, rec)], 1))
    in_u, in_y = in_cols[:, :wide], in_cols[:, wide:]
    x_own = block_input[0]
    x_blocks = gather_seq(x_own)
    x_all = jnp.concatenate(x_blocks, 0)
    c_own = after(out_cotangent[0], x_blocks[1])
    c_blocks = gather_seq(c_own)
    c_all = jnp.concatenate(c_blocks, 0)
    fine = hidden // devices // members
    part = min(384, hidden // members)
    per_part = part // fine
    parts = hidden // members // part
    cut = after(mlp_weight, x_blocks[1]).reshape(-1, 2, parts, per_part, members, fine)
    cut = lax.dynamic_index_in_dim(cut, mine, 4, keepdims=False)
    cut = cut.transpose(0, 2, 1, 3, 4).reshape(mlp_weight.shape[0], -1)
    normed = after(rms_low(x_all.astype(f32), norm_gain), cut)
    out_piece = model // members
    out_cols = gather_group(
        after(lax.dynamic_slice_in_dim(out_weight, mine * out_piece, out_piece, 1), in_cols, normed)
    )
    def rows_for(value, k):
        start, common = first_of(mine ^ k)
        return jnp.concatenate(
            [
                lax.dynamic_slice_in_dim(value, start * head, 2 * head, 0),
                lax.dynamic_slice_in_dim(
                    value, common * head + ((mine ^ k) % 2) * half, half, 0
                ),
            ],
            0,
        )

    out_rows = jnp.zeros((own, model), bf16)
    for k in range(members):
        piece = rows_for(out_cols, k)
        if k:
            piece = swap(piece, k)
        out_rows = lax.dynamic_update_slice_in_dim(out_rows, piece, (mine ^ k) * out_piece, 1)

    u = jnp.dot(normed, in_u, preferred_element_type=f32).reshape(members, tokens, wide)
    u = after(u, c_blocks[1], c_blocks[2])
    y = jnp.dot(normed, in_y, preferred_element_type=f32).reshape(members, tokens, own)
    lead = taps - 1
    rim = jnp.pad(shift(u[:, tokens - lead :], 1), ((0, 0), (8 - lead, 0), (0, 0)))
    odd_flag = odd.astype(jnp.int32).reshape(1)
    cw = widen(conv_weight)
    cb = widen(conv_bias)[None]
    gb = owned(gate_bias)
    soft = -8.0 * owned(jax.nn.softplus(decay_param))[None]
    gw = lax.dynamic_slice_in_dim(gate_weight, first, 2, 1)
    gs = lax.dynamic_slice(
        gate_weight, (0, shared, 0, odd * half), (2, 1, head, half)
    )[:, 0]
    rows = members * tokens
    full = jax.ShapeDtypeStruct((members, tokens, own), f32)
    conv, recur, gate, decay, state_local, decay_cum = pl.pallas_call(
        functools.partial(forward_kernel, head),
        grid=(members,),
        in_specs=[
            SCALAR,
            per_seq(tokens, wide),
            per_seq(8, wide),
            whole(taps, wide),
            whole(1, wide),
            whole(2, 2, head, head),
            whole(2, head, half),
            whole(2, own),
            whole(1, own),
        ],
        out_specs=[per_seq(tokens, wide)] + [per_seq(tokens, own)] * 5,
        out_shape=[jax.ShapeDtypeStruct((members, tokens, wide), f32)] + [full] * 5,
        scratch_shapes=[
            pltpu.VMEM((tokens + 8, wide), f32),
            pltpu.VMEM((tokens, wide), bf16),
            pltpu.VMEM((2, tokens, own), f32),
        ],
        compiler_params=params("arbitrary"),
        cost_estimate=cost(14),
        name="recurrence_forward",
    )(odd_flag, u, rim, cw, cb, gw, gs, gb, soft)
    down_rows = gather_group(
        after(
            lax.dynamic_slice_in_dim(down_weight, mine * fine, fine, 0), out_cols, u
        )
    )
    carried = entering(decay_cum[:, -1], state_local[:, -1], 1)
    arrived = carried
    carried = after(carried, out_rows)
    carried8 = jnp.broadcast_to(carried[:, None], (members, 8, own))
    h, merged = pl.pallas_call(
        merge_kernel,
        grid=(members,),
        in_specs=[per_seq(tokens, own)] * 2 + [per_seq(8, own), per_seq(tokens, own)],
        out_specs=[per_seq(tokens, own)] * 2,
        out_shape=[full, jax.ShapeDtypeStruct((members, tokens, own), bf16)],
        compiler_params=params("arbitrary"),
        cost_estimate=cost(14),
        name="recurrence_merge",
    )(state_local, decay_cum, carried8, y)
    partial = jnp.dot(merged.reshape(rows, own), out_rows, preferred_element_type=f32)
    partial = partial.astype(bf16)
    mlp_cols = gather_group(after(cut, down_rows, out_rows, arrived))
    partial = lax.optimization_barrier(partial).reshape(members, tokens, model)
    x32 = x_own.astype(f32)
    grad_hidden = lax.dot_general(
        c_all, down_rows, (((1,), (1,)), ((), ())), preferred_element_type=f32
    )
    resid = after(x32 + scatter_seq(partial), grad_hidden)
    normed2 = jnp.concatenate(gather_seq(rms_low(resid, mlp_gain)), 0)

    width = parts * part
    hidden_low, grad_gu = pl.pallas_call(
        mlp_kernel,
        grid=(parts,),
        in_specs=[
            whole(rows, model),
            pl.BlockSpec((model, 2 * part), lambda i: (0, i)),
            pl.BlockSpec((rows, part), lambda i: (0, i)),
        ],
        out_specs=[
            pl.BlockSpec((rows, part), lambda i: (0, i)),
            pl.BlockSpec((rows, 2 * part), lambda i: (0, i)),
        ],
        out_shape=[
            jax.ShapeDtypeStruct((rows, width), bf16),
            jax.ShapeDtypeStruct((rows, 2 * width), bf16),
        ],
        compiler_params=params("arbitrary"),
        cost_estimate=pl.CostEstimate(
            flops=4 * rows * model * width,
            bytes_accessed=rows * model * 2 + model * width * 4 + rows * width * 10,
            transcendentals=rows * width,
        ),
        name="mlp",
    )(normed2, mlp_cols, grad_hidden)
    across = (((1,), (1,)), ((), ()))
    down = (((0,), (0,)), ((), ()))
    down_part = lax.dot_general(hidden_low, c_all, down, preferred_element_type=f32).astype(bf16)
    down_sum = scatter_group(down_part)
    partial = lax.dot_general(
        after(grad_gu, down_part), mlp_cols, across, preferred_element_type=f32
    ).astype(bf16)
    mlp_part = lax.dot_general(
        normed2, after(grad_gu, partial), down, preferred_element_type=f32
    ).astype(bf16)
    grad_normed2 = scatter_seq(lax.optimization_barrier(partial).reshape(members, tokens, model))
    final = jnp.dot(
        after(hidden_low, mlp_part), down_rows, preferred_element_type=f32
    ).astype(bf16)
    grad_normed2 = after(grad_normed2, final)
    grad_resid_norm, mlp_gain_grad = rms_back(resid, mlp_gain, grad_normed2)
    grad_resid = c_own.astype(f32) + grad_resid_norm
    grad_resid_all = jnp.concatenate(gather_seq(grad_resid.astype(bf16)), 0)
    mlp_sum = scatter_group(after(mlp_part, down_sum, grad_normed2))

    final = after(final, grad_resid_all).reshape(members, tokens, model)
    final_hop = first_hop(final[3])
    block_out = (resid + scatter_seq(final, final_hop)).astype(bf16)[None]
    grad_merged = lax.dot_general(
        grad_resid_all, out_rows, (((1,), (1,)), ((), ())), preferred_element_type=f32
    ).reshape(members, tokens, own)
    grad_merged = after(grad_merged, *final_hop)
    down_first = after(down_sum, *final_hop)
    down_hop = swap(down_first, 1), swap(down_first, 2)
    grad_h, grad_y, back_local, back_cum = pl.pallas_call(
        adjoint_kernel,
        grid=(members,),
        in_specs=[per_seq(tokens, own)] * 4,
        out_specs=[per_seq(tokens, own)] * 4,
        out_shape=[full, jax.ShapeDtypeStruct((members, tokens, own), bf16), full, full],
        compiler_params=params("arbitrary"),
        cost_estimate=cost(10),
        name="recurrence_adjoint",
    )(grad_merged, h, y, decay)
    incoming = entering(back_cum[:, 0], back_local[:, 0], -1)
    incoming8 = jnp.broadcast_to(incoming[:, None], (members, 8, own))
    grad_proj, tail, owed, small, tap_sums, gw_grad, gs_grad = pl.pallas_call(
        functools.partial(backward_kernel, head),
        grid=(members,),
        in_specs=[
            SCALAR,
            *[per_seq(tokens, own)] * 4,
            per_seq(8, own),
            per_seq(8, own),
            *[per_seq(tokens, own)] * 3,
            *[per_seq(tokens, wide)] * 2,
            per_seq(tokens, own),
            per_seq(8, wide),
            whole(taps, wide),
            whole(2, 2, head, head),
            whole(2, head, half),
            whole(1, own),
        ],
        out_specs=[
            per_seq(tokens, wide + own),
            per_seq(8, wide),
            per_seq(8, wide),
            whole(8, own),
            whole(8, wide),
            whole(2, 2, head, head),
            whole(2, head, half),
        ],
        out_shape=[
            jax.ShapeDtypeStruct((members, tokens, wide + own), bf16),
            jax.ShapeDtypeStruct((members, 8, wide), f32),
            jax.ShapeDtypeStruct((members, 8, wide), f32),
            jax.ShapeDtypeStruct((8, own), f32),
            jax.ShapeDtypeStruct((8, wide), f32),
            jax.ShapeDtypeStruct((2, 2, head, head), f32),
            jax.ShapeDtypeStruct((2, head, half), f32),
        ],
        scratch_shapes=[
            pltpu.VMEM((tokens + 8, wide), f32),
            pltpu.VMEM((tokens + 8, own), f32),
            pltpu.VMEM((tokens + 8, own), f32),
            pltpu.VMEM((tokens, wide), bf16),
            pltpu.VMEM((2, tokens, own), bf16),
            pltpu.VMEM((tokens + 8, wide), f32),
        ],
        compiler_params=params("arbitrary"),
        cost_estimate=cost(19),
        name="recurrence_backward",
    )(
        odd_flag, back_local, back_cum, grad_h, h, carried8, incoming8, recur, gate,
        decay, conv, u, grad_y, rim, cw, gw, gs, soft,
    )
    tail = (tail + shift(owed, -1)).astype(bf16)
    grad_proj = lax.dynamic_update_slice(grad_proj, tail, (0, tokens - 8, 0))
    grad_proj = grad_proj.reshape(rows, wide + own)
    out_part = lax.dot_general(
        merged.reshape(rows, own), grad_resid_all, down, preferred_element_type=f32
    ).astype(bf16)
    pieces = []
    for k in range(members):
        piece = lax.dynamic_slice_in_dim(out_part, (mine ^ k) * out_piece, out_piece, 1)
        pieces.append(swap(piece, k) if k else piece)
    pieces = jnp.stack(pieces)
    out_terms = []
    for member in range(members):
        piece = lax.dynamic_index_in_dim(pieces, mine ^ member, 0, keepdims=False)
        cut_at = 2 * head if member % 2 else 0
        out_terms += [piece[cut_at:], piece[:cut_at]]
    out_terms = jnp.concatenate(out_terms, 0)
    gate_terms = jnp.concatenate([gw_grad[:, 0], gw_grad[:, 1], gs_grad], -1).reshape(-1, own)
    decay_terms = small[2:3] * (-8.0) * owned(jax.nn.sigmoid(decay_param))[None]
    sizes = ((taps + 1) * wide, 3 * own, model)
    small_terms = jnp.concatenate(
        [
            tap_sums[: taps + 1].reshape(-1),
            small[:2].reshape(-1),
            decay_terms.reshape(-1),
            mlp_gain_grad,
        ]
    )
    small_rows = 64
    small_terms = jnp.pad(small_terms, (0, small_rows * own - small_terms.shape[0]))
    terms = jnp.concatenate([gate_terms, small_terms.reshape(small_rows, own)], 0).astype(bf16)
    group_terms = total_group(terms)
    partial = lax.dot_general(
        after(grad_proj, out_terms, *down_hop, group_terms), in_cols, across, preferred_element_type=f32
    )
    partial = lax.optimization_barrier(partial.astype(bf16)).reshape(members, tokens, model)
    hop = first_hop(partial[3])
    out_sum = scatter_group(after(out_terms, mlp_sum, grad_proj))
    in_part = lax.dot_general(normed, grad_proj, down, preferred_element_type=f32).astype(bf16)
    in_sum = scatter_group(after(in_part, out_sum, *hop))

    out_blocks = gather_seq(out_sum)
    grad_normed = scatter_seq(partial, (after(hop[0], out_sum), after(hop[1], out_sum)))
    mlp_late = after(mlp_sum, out_sum)
    mlp_hop = swap(mlp_late, 1), swap(mlp_late, 2)
    term_parts = gather_seq(after(group_terms, *hop))
    gate_parts = [after(piece[: 2 * head], in_sum) for piece in term_parts]
    small_parts = jnp.stack([piece[2 * head :].reshape(-1) for piece in term_parts])
    grad_input_norm, norm_gain_grad = rms_back(x32, norm_gain, grad_normed)
    input_grad = (grad_resid + grad_input_norm)[None]

    mlp_blocks = gather_seq(mlp_late, mlp_hop)
    mlp_grad = spread(
        functools.partial(spread_mlp_kernel, (parts, per_part, fine)),
        mine,
        mlp_blocks,
        2 * hidden,
        "spread_mlp",
    )
    out_parts = jnp.stack(out_blocks)
    out_grad = jnp.concatenate(
        [lax.dynamic_index_in_dim(out_parts, mine ^ a, 0, keepdims=False) for a in range(members)],
        1,
    ).astype(f32)
    down_parts = jnp.stack(gather_seq(down_sum, down_hop))
    down_grad = jnp.concatenate(
        [lax.dynamic_index_in_dim(down_parts, mine ^ a, 0, keepdims=False) for a in range(members)],
        0,
    ).astype(f32)
    gate_grad = jnp.zeros((2, heads, head, head), f32)
    for k in range(members):
        start, common = first_of(mine ^ k)
        block = gate_parts[k].reshape(2, head, own).astype(f32)
        pair = block[:, :, : 2 * head].reshape(2, head, 2, head).transpose(0, 2, 1, 3)
        gate_grad = lax.dynamic_update_slice_in_dim(gate_grad, pair, start, 1)
        if k % 2 == 0:
            other = gate_parts[k + 1].reshape(2, head, own).astype(f32)
            halves = jnp.where(
                odd == 1,
                jnp.concatenate([other[..., 2 * head :], block[..., 2 * head :]], -1),
                jnp.concatenate([block[..., 2 * head :], other[..., 2 * head :]], -1),
            )
            gate_grad = lax.dynamic_update_slice_in_dim(gate_grad, halves[:, None], common, 1)

    def place(value, member, wide_shared):
        start, common = first_of(member)
        at = common * head if wide_shared else common * head + (member % 2) * half
        out = jnp.zeros((value.shape[0], rec), f32)
        out = lax.dynamic_update_slice_in_dim(out, value[:, : 2 * head], start * head, 1)
        return lax.dynamic_update_slice_in_dim(out, value[:, 2 * head :], at, 1)

    tap_grads, own_grads, mlp_gain_grad = 0.0, 0.0, 0.0
    for member in range(members):
        piece = lax.dynamic_index_in_dim(small_parts, mine ^ member, 0, keepdims=False).astype(f32)
        one, two, three, _ = jnp.split(
            piece, (sizes[0], sizes[0] + sizes[1], sizes[0] + sizes[1] + sizes[2])
        )
        tap_grads = tap_grads + place(one.reshape(-1, wide), member, True)
        own_grads = own_grads + place(two.reshape(-1, own), member, False)
        mlp_gain_grad = mlp_gain_grad + three
    norm_gain_grad = total(after(norm_gain_grad, *mlp_blocks).reshape(-1, 128)).reshape(-1)
    in_grad = spread(
        functools.partial(spread_in_kernel, head), mine, gather_seq(after(in_sum, *mlp_hop, *out_blocks, *term_parts)), 2 * rec, "spread_in"
    )

    return (
        block_out,
        input_grad,
        norm_gain_grad,
        in_grad,
        tap_grads[1:],
        tap_grads[0],
        gate_grad,
        own_grads[:2],
        own_grads[2],
        out_grad,
        mlp_gain_grad,
        mlp_grad,
        down_grad,
    )


def solution(mesh):
    tokens = P("seq", "group", None)
    rows = P("group", None)
    in_specs = (tokens, tokens, P(), rows, P(), P(), P(), P(), P(), rows, P(), rows, rows)
    out_specs = (tokens, tokens, P(), rows, P(), P(), P(), P(), P(), rows, P(), rows, rows)
    return jax.shard_map(shards, mesh=mesh, in_specs=in_specs, out_specs=out_specs, check_vma=False)
```
